32 devices in a mesh: gx: 4 (over z), gy: 4 (over y, x), gz: 2 (over core).
Axes of the slice: x: 2, y: 2, z: 4, core: 2. Of those that a mesh axis runs over, the one named last changes fastest.
Arguments:
- density: float32 [128, 64, 256], P('gx', 'gy', 'gz'), may hold values from 0.5 to 2
- momentum: float32 [2, 128, 64, 256], P(None, 'gx', 'gy', 'gz'), may hold values from -3 to 3
- lower_face: float32 [128], P('gx'), may hold values from 2048 to 8192
Outputs:
- updated: float32 [3, 128, 64, 256], P(None, 'gx', 'gy', 'gz')
The draws below stay inside these ranges and needn't reach their ends.
All inputs are finite; a program needn't handle non-finite values.
Results may differ from the reference program's by a relative error of at most 0.0003.
Values sent between devices are 32-bit elements; how exact they have to be, the bound alone decides.
No kernel may reach another device: no remote copies, remote signals or barrier semaphores. Data moves between devices by JAX's collectives and lax.ppermute only.
A program may use at most 64 MiB of HBM per device.

```python
import math
import jax
import jax.numpy as jnp
from jax import lax

NX = 128
NY = 64
NZ = 256


def steps_of(own_key, extent, shards, low, largest):
    def one(axis_at, blocks):
        heights = jax.random.uniform(jax.random.fold_in(jax.random.fold_in(own_key, 6), axis_at), (blocks,), jnp.float32, low / len(shards), largest / len(shards))
        return jnp.repeat(jnp.exp(heights), extent[axis_at] // blocks).reshape((-1,) + (1,) * (len(extent) - axis_at - 1))

    factor_of = one(*shards[0])
    for cut in shards[1:]:
        factor_of = factor_of * one(*cut)
    return factor_of


def gaussian(stream_key, dims, width, limit, shards=(), kind=jnp.bfloat16):
    array = jax.random.normal(stream_key, dims, jnp.float32) * width
    if len(shards) > 0:
        array = steps_of(stream_key, dims, shards, -0.22, 0.18) * array
    return jnp.clip(array, min=-limit, max=limit).astype(kind)


def setup_inputs(seed: int = 0) -> dict:
    arg_keys = jax.random.split(jax.random.key(seed), 4)
    density = jnp.clip(0.5 + 1.5 * jax.random.uniform(arg_keys[0], (NX, NY, NZ), jnp.float32) ** steps_of(arg_keys[0], (NX, NY, NZ), ((0, 4), (1, 4), (2, 2)), -0.2, 0.2), 0.5, 2.0)
    momentum = gaussian(arg_keys[1], (2, NX, NY, NZ), 0.5, 3.0, ((1, 4), (2, 4), (3, 2)), jnp.float32)
    lower_face = jnp.clip(jnp.exp(math.log(8192.0) - 1.3862944 * jax.random.uniform(arg_keys[2], (NX,), jnp.float32) ** steps_of(arg_keys[2], (NX,), ((0, 4),), -0.2, 0.2)), 2048.0, 8192.0)
    return dict(density=density, momentum=momentum, lower_face=lower_face)


time_step = 0.2


def central_sixth(field, axis):
    def diff(k):
        return jnp.roll(field, -k, axis) - jnp.roll(field, k, axis)
    return (45.0 * diff(1) - 9.0 * diff(2) + diff(3)) / 60.0


def reference(density, momentum, lower_face):
    state = jnp.concatenate([density[None], momentum], 0)
    flux_y = state * (state[1] / state[0])[None]
    flux_z = state * (state[2] / state[0])[None]
    rhs = state - time_step * (central_sixth(flux_y, 2) + central_sixth(flux_z, 3))
    upper = jnp.concatenate([lower_face[1:], lower_face[-1:]])
    diagonal = 1.0 + lower_face + upper
    position = jnp.arange(lower_face.shape[0], dtype=jnp.int32)
    below = jnp.where(position == 0, jnp.zeros_like(lower_face), -lower_face)
    above = -upper

    def coef_step(carry, items):
        sub, dia, sup = items
        denom = dia - sub * carry
        value = sup / denom
        return value, (value, denom)

    start = jnp.zeros((), jnp.float32)
    _, (primes, denoms) = lax.scan(coef_step, start, (below, diagonal, above))
    moved = jnp.moveaxis(rhs, 1, 0)

    def fwd_step(carry, items):
        sub, denom, row = items
        value = (row - sub * carry) / denom
        return value, value

    zero_row = jnp.zeros(moved.shape[1:], jnp.float32)
    _, dprime = lax.scan(fwd_step, zero_row, (below, denoms, moved))

    def back_step(carry, items):
        prime, row = items
        value = row - prime * carry
        return value, value

    _, solved = lax.scan(back_step, zero_row, (primes, dprime), reverse=True)
    return jnp.moveaxis(solved, 0, 1)
```

```python
import functools

import jax
import jax.numpy as jnp
from jax import lax
from jax.experimental import pallas as pl
from jax.experimental.pallas import tpu as pltpu
from jax.sharding import PartitionSpec as P

time_step = 0.2
scale = time_step / 60.0
ROWS = 8
F32 = jnp.float32
VMEM = pl.BlockSpec(memory_space=pltpu.VMEM)
SMEM = pl.BlockSpec(memory_space=pltpu.SMEM)
ANY = pl.BlockSpec(memory_space=pl.ANY)


def pairing(count, odd):
    pairs = []
    for low in range(1 if odd else 0, count, 2):
        high = (low + 1) % count
        pairs += [(low, high), (high, low)]
    return pairs


def partner_by(count, step):
    return [(i, i ^ step) for i in range(count)]


def rows_of(block):
    return block.reshape(block.shape[0] * block.shape[1], block.shape[2])


def shifted_z(own, low, high, k):
    nz = own.shape[-1]
    if nz % 128 == 0:
        lane = lax.broadcasted_iota(jnp.int32, own.shape, own.ndim - 1)
        if k > 0:
            return pltpu.roll(jnp.where(lane < k, high, own), nz - k, own.ndim - 1)
        return pltpu.roll(jnp.where(lane >= nz + k, low, own), -k, own.ndim - 1)
    if k > 0:
        return jnp.concatenate([own[..., k:], high[..., :k]], -1)
    return jnp.concatenate([low[..., nz + k :], own[..., : nz + k]], -1)


def sixth(take):
    return 45.0 * (take(1) - take(-1)) - 9.0 * (take(2) - take(-2)) + (take(3) - take(-3))


def sixth_z(own, low, high):
    return sixth(lambda k: shifted_z(own, low, high, k))


def join(left, right):
    inv_delta = 1.0 / (right[5] + right[2] + left[3])
    jump = (right[0] - left[1]) * inv_delta
    from_in = left[4] * inv_delta
    from_out = right[4] * inv_delta
    group = (
        left[0] + left[4] * jump,
        right[1] - right[4] * jump,
        left[2] - left[4] * from_in,
        right[3] - right[4] * from_out,
        left[4] * from_out,
        left[5],
        right[6],
    )
    return group, (jump, from_in, from_out)


def pick(cond, yes, no):
    return tuple(jnp.where(cond, a, b) for a, b in zip(yes, no))


def join_own(is_left, own, other, forms):
    left = pick(is_left, own, other)
    right = pick(is_left, other, own)
    group, (jump, from_in, from_out) = join(left, right)
    new = []
    for c0, c1, c2 in forms:
        through = jnp.where(is_left, c2, c1)
        new.append(
            (
                c0 + through * jump,
                jnp.where(is_left, c1, 0.0) + through * from_in,
                jnp.where(is_left, 0.0, c2) + through * from_out,
            )
        )
    return group, new


def closing(is_left, group, forms):
    first, last, alpha, beta, m, inv_first, inv_last = group
    kappa = 1.0 / jnp.where(is_left, inv_first + alpha, inv_last + beta)
    outer = jnp.where(is_left, first, -last) * kappa
    gain = kappa * m
    facing = jnp.where(is_left, last - m * outer, first + m * outer)
    resist = jnp.where(is_left, beta, alpha + inv_first) - m * gain
    out = []
    for c0, c1, c2 in forms:
        far = jnp.where(is_left, c1, c2)
        near = jnp.where(is_left, c2, c1)
        out.append((c0 + far * outer, far * gain + near))
    return facing, resist, out


def put_scalars(ref, block, values):
    for row, value in enumerate(values):
        ref[block, row : row + 1] = value


def get_scalars(ref, block, count):
    return [ref[block, row : row + 1] for row in range(count)]


def store_group(ref, group, tiles):
    for f in range(3):
        ref[f * tiles : (f + 1) * tiles] = group[0][f]
        ref[(3 + f) * tiles : (4 + f) * tiles] = group[1][f]
    put_scalars(ref, 6 * tiles, group[2:])


def load_group(ref, tiles):
    shape = (3, tiles) + ref.shape[1:]
    first = ref[: 3 * tiles].reshape(shape)
    last = ref[3 * tiles : 6 * tiles].reshape(shape)
    return (first, last, *get_scalars(ref, 6 * tiles, 5))


def store_closing(msg_ref, own_ref, facing, resist, out, tiles):
    for f in range(3):
        msg_ref[f * tiles : (f + 1) * tiles] = facing[f]
        own_ref[f * tiles : (f + 1) * tiles] = out[0][0][f]
        own_ref[(3 + f) * tiles : (4 + f) * tiles] = out[1][0][f]
    put_scalars(msg_ref, 3 * tiles, [resist])
    put_scalars(own_ref, 6 * tiles, [out[0][1], out[1][1]])


def store_forms(ref, forms, tiles):
    for f in range(3):
        ref[f * tiles : (f + 1) * tiles] = forms[0][0][f]
        ref[(3 + f) * tiles : (4 + f) * tiles] = forms[1][0][f]
    put_scalars(ref, 6 * tiles, [*forms[0][1:], *forms[1][1:]])


def load_forms(ref, tiles):
    shape = (3, tiles) + ref.shape[1:]
    scalars = get_scalars(ref, 6 * tiles, 4)
    return [
        (ref[: 3 * tiles].reshape(shape), scalars[0], scalars[1]),
        (ref[3 * tiles : 6 * tiles].reshape(shape), scalars[2], scalars[3]),
    ]


def first_kernel(
    faces, density, momentum,
    flux_y, flux_z, sums, small_a, small_b, edge_a, edge_b, coefs, scalars,
    rho_v, mom_v, sems,
):
    nx, tiles, _, nz = density.shape
    ny = tiles * ROWS
    copies = [
        pltpu.make_async_copy(density, rho_v, sems.at[0]),
        pltpu.make_async_copy(momentum, mom_v, sems.at[1]),
    ]
    for copy in copies:
        copy.start()
    tile = (ROWS, nz)
    inv = [1.0 / jnp.full(tile, faces[i], F32) for i in range(nx)]
    phi = [jnp.ones(tile, F32)]
    flux = phi[0]
    for i in range(1, nx):
        phi.append(phi[-1] + flux * inv[i])
        flux = flux + phi[-1]
    m = 1.0 / flux
    psi = [jnp.ones(tile, F32)]
    flux = psi[0]
    for i in range(nx - 1, 0, -1):
        psi.append(psi[-1] + flux * inv[i])
        flux = flux + psi[-1]
    psi = psi[::-1]
    for i in range(nx):
        coefs[i] = phi[i]
        coefs[nx + i] = psi[i] * m
    scalars[0:1] = (psi[0] * m)[0:1]
    scalars[1:2] = (phi[nx - 1] * m)[0:1]
    scalars[2:3] = m[0:1]
    scalars[3:4] = inv[0][0:1]
    scalars[4:5] = inv[nx - 1][0:1]
    scalars[5:8] = jnp.zeros((3, nz), F32)
    for copy in copies:
        copy.wait()
    total = [[None] * 9, [None] * 9]
    for x in range(nx):
        rho, m0, m1 = rho_v[x], mom_v[0, x], mom_v[1, x]
        inv_rho = 1.0 / rho
        v0, v1 = m0 * inv_rho, m1 * inv_rho
        cross = m0 * v1
        values = (rho, m0, m1, m0, m0 * v0, cross, m1, cross, m1 * v1)
        for f in range(3):
            flux_y[f, x] = values[3 + f]
            flux_z[f, x] = values[6 + f]
        for side, weight in enumerate((coefs[nx + x], coefs[x])):
            for k, value in enumerate(values):
                term = value * weight
                total[side][k] = term if x == 0 else total[side][k] + term
    for side in range(2):
        for f in range(3):
            at = (3 * side + f) * tiles
            sums[at : at + tiles] = total[side][f]
            sums[6 * tiles + at : 6 * tiles + at + tiles] = total[side][3 + f]
            flux_z[3, (3 * side + f)] = total[side][6 + f]
    odd = lax.rem(lax.axis_index("gy"), 2)
    for ref_small, ref_edge, high in ((small_a, edge_a, 1 - odd), (small_b, edge_b, odd)):
        for k in range(6):
            at = (6 + k) * tiles + high * (tiles - 1)
            ref_small[k] = sums[pl.ds(at, 1)][0]
        start = high * (ny - 3)
        for f in range(3):
            for x in range(nx):
                for k in range(3):
                    ref_edge[3 * f + k, x : x + 1] = flux_y.at[f, x].reshape(ny, nz)[pl.ds(start + k, 1)]


def halos_y(is_odd, from_a, from_b):
    low = jnp.where(is_odd, from_a, from_b)
    high = jnp.where(is_odd, from_b, from_a)
    return low, high


def second_kernel(
    stages, nx, sums, scalars, zsum, zsum_low, zsum_high, small_a, small_b, msg, own, pad
):
    nblocks, _, nz = sums.shape
    tiles = nblocks // 12
    ny = tiles * ROWS
    is_odd = lax.rem(lax.axis_index("gy"), 2) == 1
    low, high = halos_y(is_odd, small_a[...], small_b[...])
    alpha, beta, m, inv_first, inv_last = [scalars[i : i + 1] for i in range(5)]
    values = []
    for k in range(6):
        pad[k, 0:ROWS] = low[k]
        pad[k, ROWS : ROWS + ny] = sums[(6 + k) * tiles : (7 + k) * tiles].reshape(ny, nz)
        pad[k, ROWS + ny : 2 * ROWS + ny] = high[k]
        dy = sixth(lambda s: pad[k, ROWS + s : ROWS + s + ny])
        zs = [r[k].reshape(ny, nz) for r in (zsum, zsum_low, zsum_high)]
        dz = sixth_z(*zs)
        state = sums[k * tiles : (k + 1) * tiles].reshape(ny, nz)
        values.append((state - scale * (dy + dz)).reshape(tiles, ROWS, nz))
    first = jnp.stack(values[:3])
    last = jnp.stack(values[3:]) * m
    group = (first, last, alpha, beta, m, inv_first, inv_last)
    forms = [(0.0, 1.0, 0.0), (0.0, 0.0, 1.0)]
    if stages == 1:
        is_left = lax.rem(lax.axis_index("gx"), 2) == 0
        zero = jnp.zeros_like(first)
        one = jnp.ones_like(alpha)
        forms = [(zero, one, 0.0 * one), (zero, 0.0 * one, one)]
        facing, resist, out = closing(is_left, group, forms)
        store_closing(msg, own, facing, resist, out, tiles)
    else:
        store_group(msg, group, tiles)


def join_kernel(stage, stages, tiles, *refs):
    if stage == 0:
        mine, other, msg, own = refs
        shape = (3, tiles) + mine.shape[1:]
        zero, one = jnp.zeros(shape, F32), jnp.ones((1, shape[-1]), F32)
        forms = [(zero, one, 0.0 * one), (zero, 0.0 * one, one)]
    else:
        mine, other, forms_ref, msg, own = refs
        forms = load_forms(forms_ref, tiles)
    at = lax.axis_index("gx")
    is_left = lax.rem(lax.div(at, 1 << stage), 2) == 0
    group, forms = join_own(is_left, load_group(mine, tiles), load_group(other, tiles), forms)
    if stage + 2 == stages:
        is_left = lax.rem(lax.div(at, 2 << stage), 2) == 0
        facing, resist, out = closing(is_left, group, forms)
        store_closing(msg, own, facing, resist, out, tiles)
    else:
        store_group(msg, group, tiles)
        store_forms(own, forms, tiles)


def last_kernel(
    stages, density, momentum, flux_y, flux_z, flux_z_low, flux_z_high, edge_a, edge_b, coefs, scalars,
    mine, other, own, updated, rho_v, mom_v, out_v, pad, rhs, sems,
):
    nx, tiles, _, nz = density.shape
    ny = tiles * ROWS
    copies = [
        pltpu.make_async_copy(density, rho_v, sems.at[0]),
        pltpu.make_async_copy(momentum, mom_v, sems.at[1]),
    ]
    for copy in copies:
        copy.start()
    is_odd = lax.rem(lax.axis_index("gy"), 2) == 1
    low, high = halos_y(is_odd, edge_a[...], edge_b[...])
    for f in range(3):
        for x in range(nx):
            pad[f, x, ROWS : ROWS + ny] = flux_y[f, x].reshape(ny, nz)
            for k in range(3):
                pad[f, x, ROWS - 3 + k : ROWS - 2 + k] = low[3 * f + k, x : x + 1]
                pad[f, x, ROWS + ny + k : ROWS + ny + k + 1] = high[3 * f + k, x : x + 1]
    is_left = lax.rem(lax.div(lax.axis_index("gx"), 1 << (stages - 1)), 2) == 0
    sign = jnp.where(is_left, 1.0, -1.0)
    inv = sign / (mine[3 * tiles, 0:1] + other[3 * tiles, 0:1])
    m = scalars[2:3]
    jin, jout = [], []
    for f in range(3):
        at = slice(f * tiles, (f + 1) * tiles)
        mid = (other[at] - mine[at]) * inv
        jin.append(own[at] + own[6 * tiles, 0:1] * mid)
        jout.append(own[(3 + f) * tiles : (4 + f) * tiles] + own[6 * tiles, 1:2] * mid)
    for copy in copies:
        copy.wait()
    outs = []
    for f in range(3):
        total = -jin[f]
        for x in range(nx):
            dy = sixth(lambda s: pad[f, x, ROWS + s : ROWS + s + ny])
            dz = sixth_z(*[r[f, x].reshape(ny, nz) for r in (flux_z, flux_z_low, flux_z_high)])
            state = rho_v[x] if f == 0 else mom_v[f - 1, x]
            r = state - scale * (dy + dz).reshape(tiles, ROWS, nz)
            rhs[x] = r
            total = total + coefs[x] * r
            out_v[f, x] = total
        total = m * jout[f]
        for x in range(nx - 1, -1, -1):
            out_v[f, x] = coefs[nx + x] * out_v[f, x] + coefs[x] * total
            if x > 0:
                total = total + coefs[nx + x] * rhs[x]
        copy = pltpu.make_async_copy(out_v.at[f], updated.at[f], sems.at[2 + f])
        copy.start()
        outs.append(copy)
    for copy in outs:
        copy.wait()


def params(limit=48):
    return pltpu.CompilerParams(vmem_limit_bytes=limit * 1024 * 1024)


def swap_edges(block_a, block_b, axis):
    count = lax.axis_size(axis)
    return (
        lax.ppermute(block_a, axis, pairing(count, False)),
        lax.ppermute(block_b, axis, pairing(count, True)),
    )


def on_device(density, momentum, lower_face):
    nx, ny, nz = density.shape
    tiles = ny // ROWS
    density = density.reshape(nx, tiles, ROWS, nz)
    momentum = momentum.reshape(2, nx, tiles, ROWS, nz)
    devices = lax.axis_size("gx")
    stages = (devices - 1).bit_length()
    full = lambda *lead: jax.ShapeDtypeStruct(lead + (ROWS, nz), F32)
    flux_y, flux_z, sums, small_a, small_b, edge_a, edge_b, coefs, scalars = pl.pallas_call(
        first_kernel,
        in_specs=[SMEM, ANY, ANY],
        out_specs=[VMEM] * 9,
        out_shape=[
            full(3, nx, tiles),
            full(4, nx, tiles),
            full(12 * tiles),
            full(6),
            full(6),
            jax.ShapeDtypeStruct((9, nx, nz), F32),
            jax.ShapeDtypeStruct((9, nx, nz), F32),
            full(2 * nx),
            full(),
        ],
        scratch_shapes=[
            pltpu.VMEM((nx, tiles, ROWS, nz), F32),
            pltpu.VMEM((2, nx, tiles, ROWS, nz), F32),
            pltpu.SemaphoreType.DMA((2,)),
        ],
        compiler_params=params(),
        name="fluxes",
    )(lower_face, density, momentum)
    count_z = lax.axis_size("gz")
    if count_z == 2:
        z_low = z_high = lax.ppermute(flux_z, "gz", [(0, 1), (1, 0)])
    else:
        ring = [(i, (i + 1) % count_z) for i in range(count_z)]
        z_low = lax.ppermute(flux_z, "gz", ring)
        z_high = lax.ppermute(flux_z, "gz", [(b, a) for a, b in ring])
    got_a, got_b = swap_edges(small_a, small_b, "gy")
    far_a, far_b = swap_edges(edge_a, edge_b, "gy")
    msg_shapes = [full(6 * tiles + 1), full(3 * tiles + 1)]
    msg, own = pl.pallas_call(
        functools.partial(second_kernel, stages, nx),
        in_specs=[VMEM] * 7,
        out_specs=[VMEM] * 2,
        out_shape=[msg_shapes[stages == 1], full(6 * tiles + 1)],
        scratch_shapes=[pltpu.VMEM((6, ny + 2 * ROWS, nz), F32)],
        compiler_params=params(),
        name="interface",
    )(sums, scalars, flux_z[3, :6], z_low[3, :6], z_high[3, :6], got_a, got_b)
    other = lax.ppermute(msg, "gx", partner_by(devices, 1))
    for stage in range(stages - 1):
        extra = () if stage == 0 else (own,)
        msg, own = pl.pallas_call(
            functools.partial(join_kernel, stage, stages, tiles),
            in_specs=[VMEM] * (2 + len(extra)),
            out_specs=[VMEM] * 2,
            out_shape=[msg_shapes[stage + 2 == stages], full(6 * tiles + 1)],
            compiler_params=params(),
            name="join",
        )(msg, other, *extra)
        other = lax.ppermute(msg, "gx", partner_by(devices, 2 << stage))
    updated = pl.pallas_call(
        functools.partial(last_kernel, stages),
        in_specs=[ANY, ANY] + [VMEM] * 11,
        out_specs=ANY,
        out_shape=full(3, nx, tiles),
        scratch_shapes=[
            pltpu.VMEM((nx, tiles, ROWS, nz), F32),
            pltpu.VMEM((2, nx, tiles, ROWS, nz), F32),
            pltpu.VMEM((3, nx, tiles, ROWS, nz), F32),
            pltpu.VMEM((3, nx, ny + 2 * ROWS, nz), F32),
            pltpu.VMEM((nx, tiles, ROWS, nz), F32),
            pltpu.SemaphoreType.DMA((5,)),
        ],
        compiler_params=params(),
        name="solve",
    )(density, momentum, flux_y, flux_z, z_low, z_high, far_a, far_b, coefs, scalars, msg, other, own)
    return updated.reshape(3, nx, ny, nz)


def solution(mesh):
    placed = (P("gx", "gy", "gz"), P(None, "gx", "gy", "gz"), P("gx"))
    return jax.shard_map(
        on_device, mesh=mesh, in_specs=placed, out_specs=P(None, "gx", "gy", "gz"), check_vma=False
    )
```

```python
import functools

import jax
import jax.numpy as jnp
from jax import lax
from jax.experimental import pallas as pl
from jax.experimental.pallas import tpu as pltpu
from jax.sharding import PartitionSpec as P

time_step = 0.2
scale = time_step / 60.0
ROWS = 8
F32 = jnp.float32
VMEM = pl.BlockSpec(memory_space=pltpu.VMEM)
ANY = pl.BlockSpec(memory_space=pl.ANY)
HBM = pl.BlockSpec(memory_space=pltpu.HBM)


def pairing(count, odd):
    pairs = []
    for low in range(1 if odd else 0, count, 2):
        high = (low + 1) % count
        pairs += [(low, high), (high, low)]
    return pairs


def partner_by(count, step):
    return [(i, i ^ step) for i in range(count)]


def rows_of(block):
    return block.reshape(block.shape[0] * block.shape[1], block.shape[2])


def shifted_z(own, low, high, k):
    nz = own.shape[-1]
    if nz % 128 == 0:
        lane = lax.broadcasted_iota(jnp.int32, own.shape, own.ndim - 1)
        if k > 0:
            return pltpu.roll(jnp.where(lane < k, high, own), nz - k, own.ndim - 1)
        return pltpu.roll(jnp.where(lane >= nz + k, low, own), -k, own.ndim - 1)
    if k > 0:
        return jnp.concatenate([own[..., k:], high[..., :k]], -1)
    return jnp.concatenate([low[..., nz + k :], own[..., : nz + k]], -1)


def sixth(take):
    return 45.0 * (take(1) - take(-1)) - 9.0 * (take(2) - take(-2)) + (take(3) - take(-3))


def sixth_z(own, low, high):
    return sixth(lambda k: shifted_z(own, low, high, k))


def join(left, right):
    inv_delta = 1.0 / (right[5] + right[2] + left[3])
    jump = (right[0] - left[1]) * inv_delta
    from_in = left[4] * inv_delta
    from_out = right[4] * inv_delta
    group = (
        left[0] + left[4] * jump,
        right[1] - right[4] * jump,
        left[2] - left[4] * from_in,
        right[3] - right[4] * from_out,
        left[4] * from_out,
        left[5],
        right[6],
    )
    return group, (jump, from_in, from_out)


def pick(cond, yes, no):
    return tuple(jnp.where(cond, a, b) for a, b in zip(yes, no))


def join_own(is_left, own, other, forms):
    left = pick(is_left, own, other)
    right = pick(is_left, other, own)
    group, (jump, from_in, from_out) = join(left, right)
    new = []
    for c0, c1, c2 in forms:
        through = jnp.where(is_left, c2, c1)
        new.append(
            (
                c0 + through * jump,
                jnp.where(is_left, c1, 0.0) + through * from_in,
                jnp.where(is_left, 0.0, c2) + through * from_out,
            )
        )
    return group, new


def closing(is_left, group, forms):
    first, last, alpha, beta, m, inv_first, inv_last = group
    kappa = 1.0 / jnp.where(is_left, inv_first + alpha, inv_last + beta)
    outer = jnp.where(is_left, first, -last) * kappa
    gain = kappa * m
    facing = jnp.where(is_left, last - m * outer, first + m * outer)
    resist = jnp.where(is_left, beta, alpha + inv_first) - m * gain
    out = []
    for c0, c1, c2 in forms:
        far = jnp.where(is_left, c1, c2)
        near = jnp.where(is_left, c2, c1)
        out.append((c0 + far * outer, far * gain + near))
    return facing, resist, out


def put_scalars(ref, block, values):
    for row, value in enumerate(values):
        ref[block, row : row + 1] = value


def get_scalars(ref, block, count):
    return [ref[block, row : row + 1] for row in range(count)]


def store_group(ref, group, tiles):
    for f in range(3):
        ref[f * tiles : (f + 1) * tiles] = group[0][f]
        ref[(3 + f) * tiles : (4 + f) * tiles] = group[1][f]
    put_scalars(ref, 6 * tiles, group[2:])


def load_group(ref, tiles):
    shape = (3, tiles) + ref.shape[1:]
    first = ref[: 3 * tiles].reshape(shape)
    last = ref[3 * tiles : 6 * tiles].reshape(shape)
    return (first, last, *get_scalars(ref, 6 * tiles, 5))


def store_closing(msg_ref, own_ref, facing, resist, out, tiles):
    for f in range(3):
        msg_ref[f * tiles : (f + 1) * tiles] = facing[f]
        own_ref[f * tiles : (f + 1) * tiles] = out[0][0][f]
        own_ref[(3 + f) * tiles : (4 + f) * tiles] = out[1][0][f]
    put_scalars(msg_ref, 3 * tiles, [resist])
    put_scalars(own_ref, 6 * tiles, [out[0][1], out[1][1]])


def store_forms(ref, forms, tiles):
    for f in range(3):
        ref[f * tiles : (f + 1) * tiles] = forms[0][0][f]
        ref[(3 + f) * tiles : (4 + f) * tiles] = forms[1][0][f]
    put_scalars(ref, 6 * tiles, [*forms[0][1:], *forms[1][1:]])


def load_forms(ref, tiles):
    shape = (3, tiles) + ref.shape[1:]
    scalars = get_scalars(ref, 6 * tiles, 4)
    return [
        (ref[: 3 * tiles].reshape(shape), scalars[0], scalars[1]),
        (ref[3 * tiles : 6 * tiles].reshape(shape), scalars[2], scalars[3]),
    ]


def first_kernel(
    faces, density, momentum,
    flux_y, flux_z, sums, small_a, small_b, edge_a, edge_b, coefs, scalars,
    face_s, rho_v, mom_v, sems,
):
    nx, tiles, _, nz = density.shape
    ny = tiles * ROWS
    pitch = ny + ROWS
    copies = [
        pltpu.make_async_copy(faces, face_s, sems.at[0]),
        pltpu.make_async_copy(density, rho_v, sems.at[1]),
        pltpu.make_async_copy(momentum, mom_v, sems.at[2]),
    ]
    for copy in copies:
        copy.start()
    tile = (ROWS, nz)
    for line in range(3 * nx + 1):
        flux_y[line * pitch : line * pitch + ROWS] = jnp.zeros(tile, F32)
    copies[0].wait()
    inv = [1.0 / jnp.full(tile, face_s[i], F32) for i in range(nx)]
    phi = [jnp.ones(tile, F32)]
    flux = phi[0]
    for i in range(1, nx):
        phi.append(phi[-1] + flux * inv[i])
        flux = flux + phi[-1]
    m = 1.0 / flux
    psi = [jnp.ones(tile, F32)]
    flux = psi[0]
    for i in range(nx - 1, 0, -1):
        psi.append(psi[-1] + flux * inv[i])
        flux = flux + psi[-1]
    psi = psi[::-1]
    for i in range(nx):
        coefs[i] = phi[i]
        coefs[nx + i] = psi[i] * m
    scalars[0:1] = (psi[0] * m)[0:1]
    scalars[1:2] = (phi[nx - 1] * m)[0:1]
    scalars[2:3] = m[0:1]
    scalars[3:4] = inv[0][0:1]
    scalars[4:5] = inv[nx - 1][0:1]
    scalars[5:8] = jnp.zeros((3, nz), F32)
    for copy in copies[1:]:
        copy.wait()
    total = [[None] * 9, [None] * 9]
    for x in range(nx):
        rho, m0, m1 = rho_v[x], mom_v[0, x], mom_v[1, x]
        inv_rho = 1.0 / rho
        v0, v1 = m0 * inv_rho, m1 * inv_rho
        cross = m0 * v1
        values = (rho, m0, m1, m0, m0 * v0, cross, m1, cross, m1 * v1)
        for f in range(3):
            at = (f * nx + x) * pitch + ROWS
            flux_y[at : at + ny] = values[3 + f].reshape(ny, nz)
            flux_z[f, x] = values[6 + f]
        for side, weight in enumerate((coefs[nx + x], coefs[x])):
            for k, value in enumerate(values):
                if k not in (3, 6):
                    term = value * weight
                    total[side][k] = term if x == 0 else total[side][k] + term
    for side in range(2):
        total[side][3], total[side][6] = total[side][1], total[side][2]
        for f in range(3):
            at = (3 * side + f) * tiles
            sums[at : at + tiles] = total[side][f]
            sums[6 * tiles + at : 6 * tiles + at + tiles] = total[side][3 + f]
            flux_z[3, (3 * side + f)] = total[side][6 + f]
    odd = lax.rem(lax.axis_index("gy"), 2)
    for ref_small, ref_edge, high in ((small_a, edge_a, 1 - odd), (small_b, edge_b, odd)):
        for k in range(6):
            at = (6 + k) * tiles + high * (tiles - 1)
            ref_small[k] = sums[pl.ds(at, 1)][0]
        start = ROWS + high * (ny - 3)
        for f in range(3):
            for k in range(3):
                ref_edge[3 * f + k] = flux_y[pl.ds(start + f * nx * pitch + k, nx, stride=pitch)]


def halos_y(is_odd, from_a, from_b):
    low = jnp.where(is_odd, from_a, from_b)
    high = jnp.where(is_odd, from_b, from_a)
    return low, high


def second_kernel(
    stages, sums, scalars, zsum, zsum_low, zsum_high, small_a, small_b, *refs
):
    msg, pad = refs[0], refs[-1]
    nblocks, _, nz = sums.shape
    tiles = nblocks // 12
    ny = tiles * ROWS
    is_odd = lax.rem(lax.axis_index("gy"), 2) == 1
    low, high = halos_y(is_odd, small_a[...], small_b[...])
    alpha, beta, m, inv_first, inv_last = [scalars[i : i + 1] for i in range(5)]
    values = []
    for k in range(6):
        pad[k, 0:ROWS] = low[k]
        pad[k, ROWS : ROWS + ny] = sums[(6 + k) * tiles : (7 + k) * tiles].reshape(ny, nz)
        pad[k, ROWS + ny : 2 * ROWS + ny] = high[k]
        dy = sixth(lambda s: pad[k, ROWS + s : ROWS + s + ny])
        zs = [r[k].reshape(ny, nz) for r in (zsum, zsum_low, zsum_high)]
        dz = sixth_z(*zs)
        state = sums[k * tiles : (k + 1) * tiles].reshape(ny, nz)
        values.append((state - scale * (dy + dz)).reshape(tiles, ROWS, nz))
    first = jnp.stack(values[:3])
    last = jnp.stack(values[3:]) * m
    group = (first, last, alpha, beta, m, inv_first, inv_last)
    if stages == 1:
        is_left = lax.rem(lax.axis_index("gx"), 2) == 0
        zero = jnp.zeros_like(first)
        one = jnp.ones_like(alpha)
        forms = [(zero, one, 0.0 * one), (zero, 0.0 * one, one)]
        facing, resist, out = closing(is_left, group, forms)
        store_closing(msg, refs[1], facing, resist, out, tiles)
    else:
        store_group(msg, group, tiles)


def join_kernel(stage, stages, tiles, *refs):
    if stage == 0:
        mine, other, msg, own = refs
        shape = (3, tiles) + mine.shape[1:]
        zero, one = jnp.zeros(shape, F32), jnp.ones((1, shape[-1]), F32)
        forms = [(zero, one, 0.0 * one), (zero, 0.0 * one, one)]
    else:
        mine, other, forms_ref, msg, own = refs
        forms = load_forms(forms_ref, tiles)
    at = lax.axis_index("gx")
    is_left = lax.rem(lax.div(at, 1 << stage), 2) == 0
    group, forms = join_own(is_left, load_group(mine, tiles), load_group(other, tiles), forms)
    if stage + 2 == stages:
        is_left = lax.rem(lax.div(at, 2 << stage), 2) == 0
        facing, resist, out = closing(is_left, group, forms)
        store_closing(msg, own, facing, resist, out, tiles)
    else:
        store_group(msg, group, tiles)
        store_forms(own, forms, tiles)


def rhs_kernel(density, momentum, flux_y, flux_z, flux_z_low, flux_z_high, after, rhs):
    nx, tiles, _, nz = density.shape
    ny = tiles * ROWS
    pitch = ny + ROWS
    for f in range(3):
        for x in range(nx):
            at = (f * nx + x) * pitch + ROWS
            dy = sixth(lambda s: flux_y[at + s : at + s + ny])
            dz = sixth_z(*[r[f, x].reshape(ny, nz) for r in (flux_z, flux_z_low, flux_z_high)])
            state = density[x] if f == 0 else momentum[f - 1, x]
            rhs[f, x] = state - scale * (dy + dz).reshape(tiles, ROWS, nz)


def sums_kernel(rhs, edge_a, edge_b, coefs, ahead, behind, lines):
    _, nx, tiles, _, nz = rhs.shape
    ny = tiles * ROWS
    is_odd = lax.rem(lax.axis_index("gy"), 2) == 1
    low, high = halos_y(is_odd, edge_a[...], edge_b[...])
    for f in range(3):
        for x in range(nx):
            lines[x * ny : (x + 1) * ny] = rhs[f, x].reshape(ny, nz)
        l3, l2, l1 = [low[3 * f + k] * scale for k in range(3)]
        h1, h2, h3 = [high[3 * f + k] * scale for k in range(3)]
        for row, value in (
            (0, 45.0 * l1 - 9.0 * l2 + l3),
            (1, l2 - 9.0 * l1),
            (2, l1),
            (ny - 3, -h1),
            (ny - 2, 9.0 * h1 - h2),
            (ny - 1, 9.0 * h2 - 45.0 * h1 - h3),
        ):
            at = pl.ds(row, nx, stride=ny)
            lines[at] = lines[at] + value
        total = None
        for x in range(nx):
            r = lines[x * ny : (x + 1) * ny].reshape(tiles, ROWS, nz)
            total = coefs[x] * r if x == 0 else total + coefs[x] * r
            ahead[f, x] = total
        total = jnp.zeros((tiles, ROWS, nz), F32)
        for x in range(nx - 1, -1, -1):
            behind[f, x] = total
            if x > 0:
                r = lines[x * ny : (x + 1) * ny].reshape(tiles, ROWS, nz)
                total = total + coefs[nx + x] * r


def last_kernel(stages, ahead, behind, coefs, scalars, mine, other, own, updated, out_v, sems):
    _, nx, tiles, _, nz = ahead.shape
    is_left = lax.rem(lax.div(lax.axis_index("gx"), 1 << (stages - 1)), 2) == 0
    sign = jnp.where(is_left, 1.0, -1.0)
    inv = sign / (mine[3 * tiles, 0:1] + other[3 * tiles, 0:1])
    m = scalars[2:3]
    outs = []
    for f in range(3):
        at = slice(f * tiles, (f + 1) * tiles)
        mid = (other[at] - mine[at]) * inv
        jin = own[at] + own[6 * tiles, 0:1] * mid
        jout = m * (own[(3 + f) * tiles : (4 + f) * tiles] + own[6 * tiles, 1:2] * mid)
        for x in range(nx):
            out_v[f, x] = coefs[nx + x] * (ahead[f, x] - jin) + coefs[x] * (behind[f, x] + jout)
        copy = pltpu.make_async_copy(out_v.at[f], updated.at[f], sems.at[f])
        copy.start()
        outs.append(copy)
    for copy in outs:
        copy.wait()


def params(limit=48):
    return pltpu.CompilerParams(vmem_limit_bytes=limit * 1024 * 1024)


def swap_edges(block_a, block_b, axis):
    count = lax.axis_size(axis)
    return (
        lax.ppermute(block_a, axis, pairing(count, False)),
        lax.ppermute(block_b, axis, pairing(count, True)),
    )


def on_device(density, momentum, lower_face):
    nx, ny, nz = density.shape
    tiles = ny // ROWS
    density = density.reshape(nx, tiles, ROWS, nz)
    momentum = momentum.reshape(2, nx, tiles, ROWS, nz)
    devices = lax.axis_size("gx")
    stages = (devices - 1).bit_length()
    full = lambda *lead: jax.ShapeDtypeStruct(lead + (ROWS, nz), F32)
    flux_y, flux_z, sums, small_a, small_b, edge_a, edge_b, coefs, scalars = pl.pallas_call(
        first_kernel,
        in_specs=[HBM] * 3,
        out_specs=[VMEM] * 9,
        out_shape=[
            jax.ShapeDtypeStruct((3 * nx * (ny + ROWS) + ROWS, nz), F32),
            full(4, nx, tiles),
            full(12 * tiles),
            full(6),
            full(6),
            jax.ShapeDtypeStruct((9, nx, nz), F32),
            jax.ShapeDtypeStruct((9, nx, nz), F32),
            full(2 * nx),
            full(),
        ],
        scratch_shapes=[
            pltpu.SMEM((nx,), F32),
            pltpu.VMEM((nx, tiles, ROWS, nz), F32),
            pltpu.VMEM((2, nx, tiles, ROWS, nz), F32),
            pltpu.SemaphoreType.DMA((3,)),
        ],
        compiler_params=params(),
        name="fluxes",
    )(*(pltpu.with_memory_space_constraint(x, pltpu.HBM) for x in (lower_face, density, momentum)))
    count_z = lax.axis_size("gz")
    if count_z == 2:
        z_low = z_high = lax.ppermute(flux_z, "gz", [(0, 1), (1, 0)])
    else:
        ring = [(i, (i + 1) % count_z) for i in range(count_z)]
        z_low = lax.ppermute(flux_z, "gz", ring)
        z_high = lax.ppermute(flux_z, "gz", [(b, a) for a, b in ring])
    got_a, got_b = swap_edges(small_a, small_b, "gy")
    far_a, far_b = swap_edges(edge_a, edge_b, "gy")
    msg_shapes = [full(6 * tiles + 1), full(3 * tiles + 1)]
    msg, *own = pl.pallas_call(
        functools.partial(second_kernel, stages),
        in_specs=[VMEM] * 7,
        out_specs=[VMEM] * (1 + (stages == 1)),
        out_shape=[msg_shapes[1], full(6 * tiles + 1)] if stages == 1 else msg_shapes[:1],
        scratch_shapes=[pltpu.VMEM((6, ny + 2 * ROWS, nz), F32)],
        compiler_params=params(),
        name="interface",
    )(sums, scalars, flux_z[3, :6], z_low[3, :6], z_high[3, :6], got_a, got_b)
    cells = 3 * nx * ny * nz
    rhs = pl.pallas_call(
        rhs_kernel,
        in_specs=[VMEM] * 6 + [ANY],
        out_specs=VMEM,
        out_shape=full(3, nx, tiles),
        compiler_params=params(),
        cost_estimate=pl.CostEstimate(flops=20 * cells, bytes_accessed=16 * cells, transcendentals=0),
        name="rhs",
    )(density, momentum, flux_y, flux_z, z_low, z_high, msg)
    other = lax.ppermute(msg, "gx", partner_by(devices, 1))
    for stage in range(stages - 1):
        msg, *own = pl.pallas_call(
            functools.partial(join_kernel, stage, stages, tiles),
            in_specs=[VMEM] * (2 + len(own)),
            out_specs=[VMEM] * 2,
            out_shape=[msg_shapes[stage + 2 == stages], full(6 * tiles + 1)],
            compiler_params=params(),
            name="join",
        )(msg, other, *own)
        other = lax.ppermute(msg, "gx", partner_by(devices, 2 << stage))
    ahead, behind = pl.pallas_call(
        sums_kernel,
        in_specs=[VMEM] * 4,
        out_specs=[VMEM] * 2,
        out_shape=[full(3, nx, tiles)] * 2,
        scratch_shapes=[pltpu.VMEM((nx * ny, nz), F32)],
        compiler_params=params(),
        cost_estimate=pl.CostEstimate(flops=6 * cells, bytes_accessed=12 * cells, transcendentals=0),
        name="sums",
    )(rhs, far_a, far_b, coefs)
    updated = pl.pallas_call(
        functools.partial(last_kernel, stages),
        in_specs=[VMEM] * 7,
        out_specs=HBM,
        out_shape=full(3, nx, tiles),
        scratch_shapes=[
            pltpu.VMEM((3, nx, tiles, ROWS, nz), F32),
            pltpu.SemaphoreType.DMA((3,)),
        ],
        compiler_params=params(),
        name="solve",
    )(ahead, behind, coefs, scalars, msg, other, own[0])
    return updated.reshape(3, nx, ny, nz)


def solution(mesh):
    placed = (P("gx", "gy", "gz"), P(None, "gx", "gy", "gz"), P("gx"))
    return jax.shard_map(
        on_device, mesh=mesh, in_specs=placed, out_specs=P(None, "gx", "gy", "gz"), check_vma=False
    )
```

```python
import functools

import jax
import jax.numpy as jnp
from jax import lax
from jax.experimental import pallas as pl
from jax.experimental.pallas import tpu as pltpu
from jax.sharding import PartitionSpec as P

time_step = 0.2
scale = time_step / 60.0
ROWS = 8
RHS_COST, SUMS_COST, JOIN_COST, EDGE_COST, FACE_COST = 60, 200, 20, 20000, 20000
F32 = jnp.float32
VMEM = pl.BlockSpec(memory_space=pltpu.VMEM)
ANY = pl.BlockSpec(memory_space=pl.ANY)
HBM = pl.BlockSpec(memory_space=pltpu.HBM)


def pairing(count, odd):
    pairs = []
    for low in range(1 if odd else 0, count, 2):
        high = (low + 1) % count
        pairs += [(low, high), (high, low)]
    return pairs


def partner_by(count, step):
    return [(i, i ^ step) for i in range(count)]


def rows_of(block):
    return block.reshape(block.shape[0] * block.shape[1], block.shape[2])


def shifted_z(own, low, high, k):
    nz = own.shape[-1]
    if nz % 128 == 0:
        lane = lax.broadcasted_iota(jnp.int32, own.shape, own.ndim - 1)
        if k > 0:
            return pltpu.roll(jnp.where(lane < k, high, own), nz - k, own.ndim - 1)
        return pltpu.roll(jnp.where(lane >= nz + k, low, own), -k, own.ndim - 1)
    if k > 0:
        return jnp.concatenate([own[..., k:], high[..., :k]], -1)
    return jnp.concatenate([low[..., nz + k :], own[..., : nz + k]], -1)


def sixth(take):
    return 45.0 * (take(1) - take(-1)) - 9.0 * (take(2) - take(-2)) + (take(3) - take(-3))


def sixth_z(own, low, high):
    return sixth(lambda k: shifted_z(own, low, high, k))


def join(left, right):
    inv_delta = 1.0 / (right[5] + right[2] + left[3])
    jump = (right[0] - left[1]) * inv_delta
    from_in = left[4] * inv_delta
    from_out = right[4] * inv_delta
    group = (
        left[0] + left[4] * jump,
        right[1] - right[4] * jump,
        left[2] - left[4] * from_in,
        right[3] - right[4] * from_out,
        left[4] * from_out,
        left[5],
        right[6],
    )
    return group, (jump, from_in, from_out)


def pick(cond, yes, no):
    return tuple(jnp.where(cond, a, b) for a, b in zip(yes, no))


def join_own(is_left, own, other, forms):
    left = pick(is_left, own, other)
    right = pick(is_left, other, own)
    group, (jump, from_in, from_out) = join(left, right)
    new = []
    for c0, c1, c2 in forms:
        through = jnp.where(is_left, c2, c1)
        new.append(
            (
                c0 + through * jump,
                jnp.where(is_left, c1, 0.0) + through * from_in,
                jnp.where(is_left, 0.0, c2) + through * from_out,
            )
        )
    return group, new


def closing(is_left, group, forms):
    first, last, alpha, beta, m, inv_first, inv_last = group
    kappa = 1.0 / jnp.where(is_left, inv_first + alpha, inv_last + beta)
    outer = jnp.where(is_left, first, -last) * kappa
    gain = kappa * m
    facing = jnp.where(is_left, last - m * outer, first + m * outer)
    resist = jnp.where(is_left, beta, alpha + inv_first) - m * gain
    out = []
    for c0, c1, c2 in forms:
        far = jnp.where(is_left, c1, c2)
        near = jnp.where(is_left, c2, c1)
        out.append((c0 + far * outer, far * gain + near))
    return facing, resist, out


def put_scalars(ref, block, values):
    for row, value in enumerate(values):
        ref[block, row : row + 1] = value


def get_scalars(ref, block, count):
    return [ref[block, row : row + 1] for row in range(count)]


def store_group(ref, group, tiles):
    for f in range(3):
        ref[f * tiles : (f + 1) * tiles] = group[0][f]
        ref[(3 + f) * tiles : (4 + f) * tiles] = group[1][f]
    put_scalars(ref, 6 * tiles, group[2:])


def load_group(ref, tiles):
    shape = (3, tiles) + ref.shape[1:]
    first = ref[: 3 * tiles].reshape(shape)
    last = ref[3 * tiles : 6 * tiles].reshape(shape)
    return (first, last, *get_scalars(ref, 6 * tiles, 5))


def store_closing(msg_ref, own_ref, facing, resist, out, tiles):
    own_ref[6 * tiles + 1 : 9 * tiles + 1] = facing.reshape((3 * tiles,) + facing.shape[2:])
    put_scalars(own_ref, 9 * tiles + 1, [resist])
    for f in range(3):
        msg_ref[f * tiles : (f + 1) * tiles] = facing[f]
        own_ref[f * tiles : (f + 1) * tiles] = out[0][0][f]
        own_ref[(3 + f) * tiles : (4 + f) * tiles] = out[1][0][f]
    put_scalars(msg_ref, 3 * tiles, [resist])
    put_scalars(own_ref, 6 * tiles, [out[0][1], out[1][1]])


def store_forms(ref, forms, tiles):
    for f in range(3):
        ref[f * tiles : (f + 1) * tiles] = forms[0][0][f]
        ref[(3 + f) * tiles : (4 + f) * tiles] = forms[1][0][f]
    put_scalars(ref, 6 * tiles, [*forms[0][1:], *forms[1][1:]])


def load_forms(ref, tiles):
    shape = (3, tiles) + ref.shape[1:]
    scalars = get_scalars(ref, 6 * tiles, 4)
    return [
        (ref[: 3 * tiles].reshape(shape), scalars[0], scalars[1]),
        (ref[3 * tiles : 6 * tiles].reshape(shape), scalars[2], scalars[3]),
    ]


def sums_at(nx, ny, side, k):
    start = 3 * nx * ny + (6 * side + k) * ny
    return slice(start, start + ny)


def pick_edges(ref_a, ref_b, take):
    odd = lax.rem(lax.axis_index("gy"), 2)
    for ref, high in ((ref_a, 1 - odd), (ref_b, odd)):
        take(ref, high)


def first_kernel(
    chunks, faces, density, momentum,
    rho_v, mom_v, flux_y, flux_z, small_b, small_a, edge_a, edge_b, coefs, scalars,
    face_s, sems,
):
    nx = faces.shape[0]
    nz = density.shape[1]
    ny = density.shape[0] // nx
    tiles = ny // ROWS
    face_copy = pltpu.make_async_copy(faces, face_s, sems.at[0])
    face_copy.start()
    step = nx * ny // chunks
    copies = []
    for c in range(chunks):
        at = pl.ds(c * step, step)
        copies.append(
            (
                pltpu.make_async_copy(density.at[at], rho_v.at[at], sems.at[1 + 2 * c]),
                pltpu.make_async_copy(momentum.at[:, at], mom_v.at[:, at], sems.at[2 + 2 * c]),
            )
        )
        for copy in copies[-1]:
            copy.start()
    tile = (ROWS, nz)
    pitch = ny + ROWS
    for line in range(3 * nx + 1):
        flux_y[line * pitch : line * pitch + ROWS] = jnp.zeros(tile, F32)
    face_copy.wait()
    inv = [1.0 / jnp.full(tile, face_s[i], F32) for i in range(nx)]
    phi = [jnp.ones(tile, F32)]
    flux = phi[0]
    for i in range(1, nx):
        phi.append(phi[-1] + flux * inv[i])
        flux = flux + phi[-1]
    m = 1.0 / flux
    psi = [jnp.ones(tile, F32)]
    flux = psi[0]
    for i in range(nx - 1, 0, -1):
        psi.append(psi[-1] + flux * inv[i])
        flux = flux + psi[-1]
    psi = psi[::-1]
    for i in range(nx):
        coefs[i] = phi[i]
        coefs[nx + i] = psi[i] * m
    scalars[0:1] = (psi[0] * m)[0:1]
    scalars[1:2] = (phi[nx - 1] * m)[0:1]
    scalars[2:3] = m[0:1]
    scalars[3:4] = inv[0][0:1]
    scalars[4:5] = inv[nx - 1][0:1]
    scalars[5:8] = jnp.zeros((3, nz), F32)
    total = [[None] * 6, [None] * 6]
    for x in range(nx):
        if x % (nx // chunks) == 0:
            for copy in copies[x // (nx // chunks)]:
                copy.wait()
        at = slice(x * ny, (x + 1) * ny)
        rho, m0, m1 = [b.reshape(tiles, ROWS, nz) for b in (rho_v[at], mom_v[0, at], mom_v[1, at])]
        inv_rho = 1.0 / rho
        v0, v1 = m0 * inv_rho, m1 * inv_rho
        values = (rho, m0, m1, m0 * v0, m0 * v1, m1 * v1)
        for side, weight in enumerate((coefs[nx + x], coefs[x])):
            for k, value in enumerate(values):
                term = weight * value
                total[side][k] = term if x == 0 else total[side][k] + term
        for f in range(3):
            start = (f * nx + x) * pitch + ROWS
            flux_y[start : start + ny] = values[(1, 3, 4)[f]].reshape(ny, nz)
            flux_z[f * nx * ny + x * ny : f * nx * ny + (x + 1) * ny] = values[(2, 4, 5)[f]].reshape(ny, nz)
    for side in range(2):
        for k in range(6):
            flux_z[sums_at(nx, ny, side, k)] = total[side][k].reshape(ny, nz)

    def take_small(ref, high):
        for side in range(2):
            for f, k in enumerate((1, 3, 4)):
                start = sums_at(nx, ny, side, k).start + high * (ny - ROWS)
                ref[3 * side + f] = flux_z[pl.ds(pl.multiple_of(start, ROWS), ROWS)]

    def take_edge(ref, high):
        sign = jnp.where(high == 1, scale, -scale)
        rows = [pl.ds(high * (ny - 1) + (1 - 2 * high) * k, nx, stride=ny) for k in range(3)]
        m0, m1, v0 = [], [], []
        for at in rows:
            m0.append(mom_v[0, at])
            m1.append(mom_v[1, at])
            v0.append(m0[-1] / rho_v[at] * sign)
        for f in range(3):
            n1, n2, n3 = [(m0[k] * sign, m0[k] * v0[k], m1[k] * v0[k])[f] for k in range(3)]
            ref[3 * f] = 45.0 * n1 - 9.0 * n2 + n3
            ref[3 * f + 1] = n2 - 9.0 * n1
            ref[3 * f + 2] = n1

    pick_edges(small_a, small_b, take_small)
    pick_edges(edge_a, edge_b, take_edge)


def halos_y(is_odd, from_a, from_b):
    low = jnp.where(is_odd, from_a, from_b)
    high = jnp.where(is_odd, from_b, from_a)
    return low, high


def second_kernel(stages, nx, ny, small_a, small_b, sums, sums_low, sums_high, scalars, *refs):
    nz = sums.shape[1]
    tiles = ny // ROWS
    pad = refs[-1]
    is_odd = lax.rem(lax.axis_index("gy"), 2) == 1
    low, high = halos_y(is_odd, small_a[...], small_b[...])
    alpha, beta, m, inv_first, inv_last = [scalars[i : i + 1] for i in range(5)]
    values = []
    for side in range(2):
        for f, (state, along_y, along_z) in enumerate(((0, 1, 2), (1, 3, 4), (2, 4, 5))):
            k = 3 * side + f
            pad[k, 0:ROWS] = low[k]
            pad[k, ROWS : ROWS + ny] = sums[sums_at(nx, ny, side, along_y)]
            pad[k, ROWS + ny : 2 * ROWS + ny] = high[k]
            dy = sixth(lambda s: pad[k, ROWS + s : ROWS + s + ny])
            dz = sixth_z(*[r[sums_at(nx, ny, side, along_z)] for r in (sums, sums_low, sums_high)])
            value = sums[sums_at(nx, ny, side, state)] - scale * (dy + dz)
            values.append(value.reshape(tiles, ROWS, nz))
    first = jnp.stack(values[:3])
    last = jnp.stack(values[3:]) * m
    group = (first, last, alpha, beta, m, inv_first, inv_last)
    if stages == 1:
        is_left = lax.rem(lax.axis_index("gx"), 2) == 0
        zero = jnp.zeros_like(first)
        one = jnp.ones_like(alpha)
        forms = [(zero, one, 0.0 * one), (zero, 0.0 * one, one)]
        facing, resist, out = closing(is_left, group, forms)
        store_closing(refs[0], refs[1], facing, resist, out, tiles)
    else:
        store_group(refs[0], group, tiles)


def join_kernel(stage, stages, tiles, *refs):
    refs = refs[:2] + refs[3:]
    if stage == 0:
        mine, other, msg, own = refs
        shape = (3, tiles) + mine.shape[1:]
        zero, one = jnp.zeros(shape, F32), jnp.ones((1, shape[-1]), F32)
        forms = [(zero, one, 0.0 * one), (zero, 0.0 * one, one)]
    else:
        mine, other, forms_ref, msg, own = refs
        forms = load_forms(forms_ref, tiles)
    at = lax.axis_index("gx")
    is_left = lax.rem(lax.div(at, 1 << stage), 2) == 0
    group, forms = join_own(is_left, load_group(mine, tiles), load_group(other, tiles), forms)
    if stage + 2 == stages:
        is_left = lax.rem(lax.div(at, 2 << stage), 2) == 0
        facing, resist, out = closing(is_left, group, forms)
        store_closing(msg, own, facing, resist, out, tiles)
    else:
        store_group(msg, group, tiles)
        store_forms(own, forms, tiles)


def rhs_kernel(nx, density, momentum, flux_y, flux_z, flux_z_low, flux_z_high, rhs):
    ny = density.shape[0] // nx
    pitch = ny + ROWS
    for f in range(3):
        for x in range(nx):
            at = (f * nx + x) * pitch + ROWS
            dy = sixth(lambda s: flux_y[at + s : at + s + ny])
            cells = slice(x * ny, (x + 1) * ny)
            lines = slice((f * nx + x) * ny, (f * nx + x + 1) * ny)
            dz = sixth_z(*[r[lines] for r in (flux_z, flux_z_low, flux_z_high)])
            state = density[cells] if f == 0 else momentum[f - 1, cells]
            rhs[f, cells] = state - scale * (dy + dz)


def add_edge(nx, rhs, edge, high):
    ny = rhs.shape[1] // nx
    for f in range(3):
        for k in range(3):
            at = pl.ds(high * (ny - 1) + (1 - 2 * high) * k, nx, stride=ny)
            rhs[f, at] = rhs[f, at] + edge[3 * f + k]


def edge_kernel(nx, rhs_in, edge_b, rhs):
    add_edge(nx, rhs, edge_b, lax.rem(lax.axis_index("gy"), 2))


def sums_kernel(nx, rhs_in, edge_a, coefs, rhs, ahead, behind):
    ny, nz = rhs.shape[1] // nx, rhs.shape[2]
    shape = (ny // ROWS, ROWS, nz)
    add_edge(nx, rhs, edge_a, 1 - lax.rem(lax.axis_index("gy"), 2))
    for f in range(3):
        total = None
        for x in range(nx):
            r = rhs[f, x * ny : (x + 1) * ny].reshape(shape)
            total = coefs[x] * r if x == 0 else total + coefs[x] * r
            ahead[f, x] = total
        total = jnp.zeros(shape, F32)
        for x in range(nx - 1, -1, -1):
            behind[f, x] = total
            if x > 0:
                r = rhs[f, x * ny : (x + 1) * ny].reshape(shape)
                total = total + coefs[nx + x] * r


def last_kernel(stages, parts, ahead, behind, coefs, scalars, other, own, updated, out_v, sems):
    _, nx, tiles, _, nz = ahead.shape
    is_left = lax.rem(lax.div(lax.axis_index("gx"), 1 << (stages - 1)), 2) == 0
    sign = jnp.where(is_left, 1.0, -1.0)
    inv = sign / (own[9 * tiles + 1, 0:1] + other[3 * tiles, 0:1])
    m = scalars[2:3]
    copies = []
    for f in range(3):
        at = slice(f * tiles, (f + 1) * tiles)
        mid = (other[at] - own[(6 + f) * tiles + 1 : (7 + f) * tiles + 1]) * inv
        jin = own[at] + own[6 * tiles, 0:1] * mid
        jout = m * (own[(3 + f) * tiles : (4 + f) * tiles] + own[6 * tiles, 1:2] * mid)
        for x in range(nx):
            out_v[f, x] = coefs[nx + x] * (ahead[f, x] - jin) + coefs[x] * (behind[f, x] + jout)
            if (x + 1) % (nx // parts) == 0:
                part = pl.ds(x + 1 - nx // parts, nx // parts)
                copy = pltpu.make_async_copy(out_v.at[f, part], updated.at[f, part], sems.at[len(copies)])
                copy.start()
                copies.append(copy)
    for copy in copies:
        copy.wait()


def params(limit=48):
    return pltpu.CompilerParams(vmem_limit_bytes=limit * 1024 * 1024)


def swap(block, axis, pairs, crossed):
    if not crossed:
        return lax.ppermute(block, axis, pairs)
    both = [(2 * a + c, 2 * b + 1 - c) for a, b in pairs for c in range(2)]
    return lax.ppermute(block, (axis, "gz"), both)


def swap_edges(block_a, block_b, crossed=False):
    count = lax.axis_size("gy")
    return (
        swap(block_a, "gy", pairing(count, False), crossed),
        swap(block_b, "gy", pairing(count, True), crossed),
    )


def swap_whole(block, axis):
    count = lax.axis_size(axis)
    if count == 2:
        got = lax.ppermute(block, axis, pairing(2, False))
        return got, got
    ring = [(i, (i + 1) % count) for i in range(count)]
    return lax.ppermute(block, axis, ring), lax.ppermute(block, axis, [(b, a) for a, b in ring])


def on_device(density, momentum, lower_face):
    nx, ny, nz = density.shape
    tiles = ny // ROWS
    cells = nx * ny
    chunks, parts = (4 if nx % 4 == 0 else 1), (2 if nx % 2 == 0 else 1)
    devices = lax.axis_size("gx")
    stages = (devices - 1).bit_length()
    crossed = lax.axis_size("gz") == 2
    full = lambda *lead: jax.ShapeDtypeStruct(lead + (ROWS, nz), F32)
    vec = lambda *lead: jax.ShapeDtypeStruct(lead + (nz,), F32)
    cost = lambda n: pl.CostEstimate(flops=n * cells * nz, bytes_accessed=n * cells * nz, transcendentals=0)
    inputs = (lower_face, density.reshape(cells, nz), momentum.reshape(2, cells, nz))
    inputs = [pltpu.with_memory_space_constraint(x, pltpu.HBM) for x in inputs]
    density, momentum, flux_y, flux_z, small_b, small_a, edge_a, edge_b, coefs, scalars = pl.pallas_call(
        functools.partial(first_kernel, chunks),
        in_specs=[HBM] * 3,
        out_specs=[VMEM] * 10,
        out_shape=[
            vec(cells),
            vec(2, cells),
            vec(3 * nx * (ny + ROWS) + ROWS),
            vec(3 * cells + 12 * ny),
            full(6),
            full(6),
            vec(9, nx),
            vec(9, nx),
            full(2 * nx),
            full(),
        ],
        scratch_shapes=[pltpu.SMEM((nx,), F32), pltpu.SemaphoreType.DMA((1 + 2 * chunks,))],
        compiler_params=params(),
        name="load",
    )(*inputs)
    got_a, got_b = swap_edges(small_a, small_b, crossed)
    far_a, far_b = swap_edges(edge_a, edge_b)
    z_low, z_high = swap_whole(flux_z, "gz")
    rhs = pl.pallas_call(
        functools.partial(rhs_kernel, nx),
        in_specs=[VMEM] * 6,
        out_specs=VMEM,
        out_shape=vec(3, cells),
        compiler_params=params(),
        cost_estimate=cost(RHS_COST),
        name="rhs",
    )(density, momentum, flux_y, flux_z, z_low, z_high)
    handled = (z_low, flux_z, flux_z) if crossed else (flux_z, z_low, z_high)
    msg_shapes = [full(6 * tiles + 1), full(3 * tiles + 1)]
    own_shapes = [full(6 * tiles + 1), full(9 * tiles + 2)]
    msg, *own = pl.pallas_call(
        functools.partial(second_kernel, stages, nx, ny),
        in_specs=[VMEM] * 6,
        out_specs=[VMEM] * (1 + (stages == 1)),
        out_shape=[msg_shapes[1], own_shapes[1]] if stages == 1 else msg_shapes[:1],
        scratch_shapes=[pltpu.VMEM((6, ny + 2 * ROWS, nz), F32)],
        compiler_params=params(),
        cost_estimate=cost(FACE_COST),
        name="interface",
    )(got_a, got_b, *handled, scalars)
    other = swap(msg, "gx", partner_by(devices, 1), crossed)
    if crossed:
        if stages == 1:
            own = [swap_whole(own[0], "gz")[0]]
        else:
            msg, _ = swap_whole(msg, "gz")
    for stage in range(stages - 1):
        closing_next = stage + 2 == stages
        msg, *own = pl.pallas_call(
            functools.partial(join_kernel, stage, stages, tiles),
            in_specs=[VMEM, VMEM, ANY] + [VMEM] * len(own),
            out_specs=[VMEM] * 2,
            out_shape=[msg_shapes[closing_next], own_shapes[closing_next]],
            compiler_params=params(),
            cost_estimate=cost(JOIN_COST),
            name="join",
        )(msg, other, rhs, *own)
        other = lax.ppermute(msg, "gx", partner_by(devices, 2 << stage))
    own = own[0]
    rhs = pl.pallas_call(
        functools.partial(edge_kernel, nx),
        in_specs=[VMEM] * 2,
        out_specs=VMEM,
        out_shape=vec(3, cells),
        input_output_aliases={0: 0},
        compiler_params=params(),
        cost_estimate=cost(EDGE_COST),
        name="edge",
    )(rhs, far_b)
    _, ahead, behind = pl.pallas_call(
        functools.partial(sums_kernel, nx),
        in_specs=[VMEM] * 3,
        out_specs=[VMEM] * 3,
        out_shape=[vec(3, cells)] + [full(3, nx, tiles)] * 2,
        input_output_aliases={0: 0},
        compiler_params=params(),
        cost_estimate=cost(SUMS_COST),
        name="sums",
    )(rhs, far_a, coefs)
    updated = pl.pallas_call(
        functools.partial(last_kernel, stages, parts),
        in_specs=[VMEM] * 6,
        out_specs=HBM,
        out_shape=full(3, nx, tiles),
        scratch_shapes=[
            pltpu.VMEM((3, nx, tiles, ROWS, nz), F32),
            pltpu.SemaphoreType.DMA((3 * parts,)),
        ],
        compiler_params=params(),
        name="solve",
    )(ahead, behind, coefs, scalars, other, own)
    return updated.reshape(3, nx, ny, nz)


def solution(mesh):
    placed = (P("gx", "gy", "gz"), P(None, "gx", "gy", "gz"), P("gx"))
    return jax.shard_map(
        on_device, mesh=mesh, in_specs=placed, out_specs=P(None, "gx", "gy", "gz"), check_vma=False
    )
```

```python
import functools

import jax
import jax.numpy as jnp
from jax import lax
from jax.experimental import pallas as pl
from jax.experimental.pallas import tpu as pltpu
from jax.sharding import PartitionSpec as P

time_step = 0.2
scale = time_step / 60.0
ROWS = 8
RHS_COST, SUMS_COST, JOIN_COST, EDGE_COST, FACE_COST, PACK_COST, HALO_COST = 60, 200, 20, 20000, 200000, 20, 20000
F32 = jnp.float32
VMEM = pl.BlockSpec(memory_space=pltpu.VMEM)
ANY = pl.BlockSpec(memory_space=pl.ANY)
HBM = pl.BlockSpec(memory_space=pltpu.HBM)


def pairing(count, odd):
    pairs = []
    for low in range(1 if odd else 0, count, 2):
        high = (low + 1) % count
        pairs += [(low, high), (high, low)]
    return pairs


def partner_by(count, step):
    return [(i, i ^ step) for i in range(count)]


def rows_of(block):
    return block.reshape(block.shape[0] * block.shape[1], block.shape[2])


def shifted_z(own, low, high, k):
    nz = own.shape[-1]
    if nz % 128 == 0:
        lane = lax.broadcasted_iota(jnp.int32, own.shape, own.ndim - 1)
        if k > 0:
            return pltpu.roll(jnp.where(lane < k, high, own), nz - k, own.ndim - 1)
        return pltpu.roll(jnp.where(lane >= nz + k, low, own), -k, own.ndim - 1)
    if k > 0:
        return jnp.concatenate([own[..., k:], high[..., :k]], -1)
    return jnp.concatenate([low[..., nz + k :], own[..., : nz + k]], -1)


def sixth(take):
    return 45.0 * (take(1) - take(-1)) - 9.0 * (take(2) - take(-2)) + (take(3) - take(-3))


def sixth_z(own, low, high):
    return sixth(lambda k: shifted_z(own, low, high, k))


def join(left, right):
    inv_delta = 1.0 / (right[5] + right[2] + left[3])
    jump = (right[0] - left[1]) * inv_delta
    from_in = left[4] * inv_delta
    from_out = right[4] * inv_delta
    group = (
        left[0] + left[4] * jump,
        right[1] - right[4] * jump,
        left[2] - left[4] * from_in,
        right[3] - right[4] * from_out,
        left[4] * from_out,
        left[5],
        right[6],
    )
    return group, (jump, from_in, from_out)


def pick(cond, yes, no):
    return tuple(jnp.where(cond, a, b) for a, b in zip(yes, no))


def join_own(is_left, own, other, forms):
    left = pick(is_left, own, other)
    right = pick(is_left, other, own)
    group, (jump, from_in, from_out) = join(left, right)
    new = []
    for c0, c1, c2 in forms:
        through = jnp.where(is_left, c2, c1)
        new.append(
            (
                c0 + through * jump,
                jnp.where(is_left, c1, 0.0) + through * from_in,
                jnp.where(is_left, 0.0, c2) + through * from_out,
            )
        )
    return group, new


def closing(is_left, group, forms):
    first, last, alpha, beta, m, inv_first, inv_last = group
    kappa = 1.0 / jnp.where(is_left, inv_first + alpha, inv_last + beta)
    outer = jnp.where(is_left, first, -last) * kappa
    gain = kappa * m
    facing = jnp.where(is_left, last - m * outer, first + m * outer)
    resist = jnp.where(is_left, beta, alpha + inv_first) - m * gain
    out = []
    for c0, c1, c2 in forms:
        far = jnp.where(is_left, c1, c2)
        near = jnp.where(is_left, c2, c1)
        out.append((c0 + far * outer, far * gain + near))
    return facing, resist, out


def put_scalars(ref, block, values):
    for row, value in enumerate(values):
        ref[block, row : row + 1] = value


def get_scalars(ref, block, count):
    return [ref[block, row : row + 1] for row in range(count)]


def store_group(ref, group, tiles):
    for f in range(3):
        ref[f * tiles : (f + 1) * tiles] = group[0][f]
        ref[(3 + f) * tiles : (4 + f) * tiles] = group[1][f]
    put_scalars(ref, 6 * tiles, group[2:])


def load_group(ref, tiles):
    shape = (3, tiles) + ref.shape[1:]
    first = ref[: 3 * tiles].reshape(shape)
    last = ref[3 * tiles : 6 * tiles].reshape(shape)
    return (first, last, *get_scalars(ref, 6 * tiles, 5))


def store_closing(msg_ref, own_ref, facing, resist, out, tiles):
    own_ref[6 * tiles + 1 : 9 * tiles + 1] = facing.reshape((3 * tiles,) + facing.shape[2:])
    put_scalars(own_ref, 9 * tiles + 1, [resist])
    for f in range(3):
        msg_ref[f * tiles : (f + 1) * tiles] = facing[f]
        own_ref[f * tiles : (f + 1) * tiles] = out[0][0][f]
        own_ref[(3 + f) * tiles : (4 + f) * tiles] = out[1][0][f]
    put_scalars(msg_ref, 3 * tiles, [resist])
    put_scalars(own_ref, 6 * tiles, [out[0][1], out[1][1]])


def store_forms(ref, forms, tiles):
    for f in range(3):
        ref[f * tiles : (f + 1) * tiles] = forms[0][0][f]
        ref[(3 + f) * tiles : (4 + f) * tiles] = forms[1][0][f]
    put_scalars(ref, 6 * tiles, [*forms[0][1:], *forms[1][1:]])


def load_forms(ref, tiles):
    shape = (3, tiles) + ref.shape[1:]
    scalars = get_scalars(ref, 6 * tiles, 4)
    return [
        (ref[: 3 * tiles].reshape(shape), scalars[0], scalars[1]),
        (ref[3 * tiles : 6 * tiles].reshape(shape), scalars[2], scalars[3]),
    ]


def sums_at(ny, side, k):
    start = (6 * side + k) * ny
    return slice(start, start + ny)


def pick_edges(ref_a, ref_b, take):
    odd = lax.rem(lax.axis_index("gy"), 2)
    for ref, high in ((ref_a, 1 - odd), (ref_b, odd)):
        take(ref, high)


def first_kernel(
    chunks, faces, density, momentum,
    rho_v, mom_v, flux_y, flux_z, sums, small_b, small_a, coefs, scalars,
    face_s, sems,
):
    nx = faces.shape[0]
    nz = density.shape[1]
    ny = density.shape[0] // nx
    tiles = ny // ROWS
    face_copy = pltpu.make_async_copy(faces, face_s, sems.at[0])
    face_copy.start()
    step = nx * ny // chunks
    copies = []
    for c in range(chunks):
        at = pl.ds(c * step, step)
        copies.append(
            (
                pltpu.make_async_copy(density.at[at], rho_v.at[at], sems.at[1 + 2 * c]),
                pltpu.make_async_copy(momentum.at[:, at], mom_v.at[:, at], sems.at[2 + 2 * c]),
            )
        )
        for copy in copies[-1]:
            copy.start()
    tile = (ROWS, nz)
    pitch = ny + ROWS
    for line in range(3 * nx + 1):
        flux_y[line * pitch : line * pitch + ROWS] = jnp.zeros(tile, F32)
    face_copy.wait()
    inv = [1.0 / jnp.full(tile, face_s[i], F32) for i in range(nx)]
    phi = [jnp.ones(tile, F32)]
    flux = phi[0]
    for i in range(1, nx):
        phi.append(phi[-1] + flux * inv[i])
        flux = flux + phi[-1]
    m = 1.0 / flux
    psi = [jnp.ones(tile, F32)]
    flux = psi[0]
    for i in range(nx - 1, 0, -1):
        psi.append(psi[-1] + flux * inv[i])
        flux = flux + psi[-1]
    psi = psi[::-1]
    for i in range(nx):
        coefs[i] = phi[i]
        coefs[nx + i] = psi[i] * m
    scalars[0:1] = (psi[0] * m)[0:1]
    scalars[1:2] = (phi[nx - 1] * m)[0:1]
    scalars[2:3] = m[0:1]
    scalars[3:4] = inv[0][0:1]
    scalars[4:5] = inv[nx - 1][0:1]
    scalars[5:8] = jnp.zeros((3, nz), F32)
    total = [[None] * 6, [None] * 6]
    for x in range(nx):
        if x % (nx // chunks) == 0:
            for copy in copies[x // (nx // chunks)]:
                copy.wait()
        at = slice(x * ny, (x + 1) * ny)
        rho, m0, m1 = [b.reshape(tiles, ROWS, nz) for b in (rho_v[at], mom_v[0, at], mom_v[1, at])]
        inv_rho = 1.0 / rho
        v0, v1 = m0 * inv_rho, m1 * inv_rho
        values = (rho, m0, m1, m0 * v0, m0 * v1, m1 * v1)
        for side, weight in enumerate((coefs[nx + x], coefs[x])):
            for k, value in enumerate(values):
                term = weight * value
                total[side][k] = term if x == 0 else total[side][k] + term
        for f in range(3):
            start = (f * nx + x) * pitch + ROWS
            flux_y[start : start + ny] = values[(1, 3, 4)[f]].reshape(ny, nz)
            flux_z[f * nx * ny + x * ny : f * nx * ny + (x + 1) * ny] = values[(2, 4, 5)[f]].reshape(ny, nz)
    for side in range(2):
        for k in range(6):
            sums[sums_at(ny, side, k)] = total[side][k].reshape(ny, nz)

    def take_small(ref, high):
        for side in range(2):
            for f, k in enumerate((1, 3, 4)):
                start = sums_at(ny, side, k).start + high * (ny - 3)
                ref[9 * side + 3 * f : 9 * side + 3 * f + 3] = sums[pl.ds(start, 3)]
        ref[18:24] = jnp.zeros((6, nz), F32)

    pick_edges(small_a, small_b, take_small)


def pack_kernel(nx, second, rho_v, mom_v, ref):
    ny = rho_v.shape[0] // nx
    odd = lax.rem(lax.axis_index("gy"), 2)
    high = odd if second else 1 - odd
    sign = jnp.where(high == 1, scale, -scale)
    rows = [pl.ds(high * (ny - 1) + (1 - 2 * high) * k, nx, stride=ny) for k in range(3)]
    m0, m1, v0 = [], [], []
    for at in rows:
        m0.append(mom_v[0, at])
        m1.append(mom_v[1, at])
        v0.append(m0[-1] / rho_v[at] * sign)
    for f in range(3):
        n1, n2, n3 = [(m0[k] * sign, m0[k] * v0[k], m1[k] * v0[k])[f] for k in range(3)]
        ref[3 * f] = 45.0 * n1 - 9.0 * n2 + n3
        ref[3 * f + 1] = n2 - 9.0 * n1
        ref[3 * f + 2] = n1


def halos_y(is_odd, from_a, from_b):
    low = jnp.where(is_odd, from_a, from_b)
    high = jnp.where(is_odd, from_b, from_a)
    return low, high


def halo_kernel(small_a, small_b, halos):
    is_odd = lax.rem(lax.axis_index("gy"), 2) == 1
    low, high = halos_y(is_odd, small_a[...], small_b[...])
    for k in range(6):
        halos[k, 0, ROWS - 3 : ROWS] = low[3 * k : 3 * k + 3]
        halos[k, 1, 0:3] = high[3 * k : 3 * k + 3]


def second_kernel(stages, halos, sums, sums_low, sums_high, scalars, *refs):
    nz = sums.shape[1]
    ny = sums.shape[0] // 12
    tiles = ny // ROWS
    pad = refs[-1]
    alpha, beta, m, inv_first, inv_last = [scalars[i : i + 1] for i in range(5)]
    values = []
    for side in range(2):
        for f, (state, along_y, along_z) in enumerate(((0, 1, 2), (1, 3, 4), (2, 4, 5))):
            k = 3 * side + f
            pad[k, 0:ROWS] = halos[k, 0]
            pad[k, ROWS : ROWS + ny] = sums[sums_at(ny, side, along_y)]
            pad[k, ROWS + ny : 2 * ROWS + ny] = halos[k, 1]
            dy = sixth(lambda s: pad[k, ROWS + s : ROWS + s + ny])
            dz = sixth_z(*[r[sums_at(ny, side, along_z)] for r in (sums, sums_low, sums_high)])
            value = sums[sums_at(ny, side, state)] - scale * (dy + dz)
            values.append(value.reshape(tiles, ROWS, nz))
    first = jnp.stack(values[:3])
    last = jnp.stack(values[3:]) * m
    group = (first, last, alpha, beta, m, inv_first, inv_last)
    if stages == 1:
        is_left = lax.rem(lax.axis_index("gx"), 2) == 0
        zero = jnp.zeros_like(first)
        one = jnp.ones_like(alpha)
        forms = [(zero, one, 0.0 * one), (zero, 0.0 * one, one)]
        facing, resist, out = closing(is_left, group, forms)
        store_closing(refs[0], refs[1], facing, resist, out, tiles)
    else:
        store_group(refs[0], group, tiles)


def join_kernel(stage, stages, tiles, *refs):
    refs = refs[:2] + refs[3:]
    if stage == 0:
        mine, other, msg, own = refs
        shape = (3, tiles) + mine.shape[1:]
        zero, one = jnp.zeros(shape, F32), jnp.ones((1, shape[-1]), F32)
        forms = [(zero, one, 0.0 * one), (zero, 0.0 * one, one)]
    else:
        mine, other, forms_ref, msg, own = refs
        forms = load_forms(forms_ref, tiles)
    at = lax.axis_index("gx")
    is_left = lax.rem(lax.div(at, 1 << stage), 2) == 0
    group, forms = join_own(is_left, load_group(mine, tiles), load_group(other, tiles), forms)
    if stage + 2 == stages:
        is_left = lax.rem(lax.div(at, 2 << stage), 2) == 0
        facing, resist, out = closing(is_left, group, forms)
        store_closing(msg, own, facing, resist, out, tiles)
    else:
        store_group(msg, group, tiles)
        store_forms(own, forms, tiles)


def rhs_kernel(nx, density, momentum, flux_y, flux_z, flux_z_low, flux_z_high, rhs):
    ny = density.shape[0] // nx
    pitch = ny + ROWS
    for f in range(3):
        for x in range(nx):
            at = (f * nx + x) * pitch + ROWS
            dy = sixth(lambda s: flux_y[at + s : at + s + ny])
            cells = slice(x * ny, (x + 1) * ny)
            lines = slice((f * nx + x) * ny, (f * nx + x + 1) * ny)
            dz = sixth_z(*[r[lines] for r in (flux_z, flux_z_low, flux_z_high)])
            state = density[cells] if f == 0 else momentum[f - 1, cells]
            rhs[f, cells] = state - scale * (dy + dz)


def add_edge(nx, rhs, edge, high):
    ny = rhs.shape[1] // nx
    for f in range(3):
        for k in range(3):
            at = pl.ds(high * (ny - 1) + (1 - 2 * high) * k, nx, stride=ny)
            rhs[f, at] = rhs[f, at] + edge[3 * f + k]


def edge_kernel(nx, rhs_in, edge_b, rhs):
    add_edge(nx, rhs, edge_b, lax.rem(lax.axis_index("gy"), 2))


def sums_kernel(nx, rhs_in, edge_a, coefs, rhs, ahead, behind):
    ny, nz = rhs.shape[1] // nx, rhs.shape[2]
    shape = (ny // ROWS, ROWS, nz)
    add_edge(nx, rhs, edge_a, 1 - lax.rem(lax.axis_index("gy"), 2))
    for f in range(3):
        total = None
        for x in range(nx):
            r = rhs[f, x * ny : (x + 1) * ny].reshape(shape)
            total = coefs[x] * r if x == 0 else total + coefs[x] * r
            ahead[f, x] = total
        total = jnp.zeros(shape, F32)
        for x in range(nx - 1, -1, -1):
            behind[f, x] = total
            if x > 0:
                r = rhs[f, x * ny : (x + 1) * ny].reshape(shape)
                total = total + coefs[nx + x] * r


def last_kernel(stages, parts, ahead, behind, coefs, scalars, other, own, updated, out_v, sems):
    _, nx, tiles, _, nz = ahead.shape
    is_left = lax.rem(lax.div(lax.axis_index("gx"), 1 << (stages - 1)), 2) == 0
    sign = jnp.where(is_left, 1.0, -1.0)
    inv = sign / (own[9 * tiles + 1, 0:1] + other[3 * tiles, 0:1])
    m = scalars[2:3]
    copies = []
    for f in range(3):
        at = slice(f * tiles, (f + 1) * tiles)
        mid = (other[at] - own[(6 + f) * tiles + 1 : (7 + f) * tiles + 1]) * inv
        jin = own[at] + own[6 * tiles, 0:1] * mid
        jout = m * (own[(3 + f) * tiles : (4 + f) * tiles] + own[6 * tiles, 1:2] * mid)
        for x in range(nx):
            out_v[f, x] = coefs[nx + x] * (ahead[f, x] - jin) + coefs[x] * (behind[f, x] + jout)
            if (x + 1) % (nx // parts) == 0:
                part = pl.ds(x + 1 - nx // parts, nx // parts)
                copy = pltpu.make_async_copy(out_v.at[f, part], updated.at[f, part], sems.at[len(copies)])
                copy.start()
                copies.append(copy)
    for copy in copies:
        copy.wait()


def params(limit=48):
    return pltpu.CompilerParams(vmem_limit_bytes=limit * 1024 * 1024)


def swap(block, axis, pairs, crossed):
    if not crossed:
        return lax.ppermute(block, axis, pairs)
    both = [(2 * a + c, 2 * b + 1 - c) for a, b in pairs for c in range(2)]
    return lax.ppermute(block, (axis, "gz"), both)


def swap_edges(block_a, block_b, crossed=False):
    count = lax.axis_size("gy")
    return (
        swap(block_a, "gy", pairing(count, False), crossed),
        swap(block_b, "gy", pairing(count, True), crossed),
    )


def swap_whole(block, axis):
    count = lax.axis_size(axis)
    if count == 2:
        got = lax.ppermute(block, axis, pairing(2, False))
        return got, got
    ring = [(i, (i + 1) % count) for i in range(count)]
    return lax.ppermute(block, axis, ring), lax.ppermute(block, axis, [(b, a) for a, b in ring])


def on_device(density, momentum, lower_face):
    nx, ny, nz = density.shape
    tiles = ny // ROWS
    cells = nx * ny
    chunks, parts = (4 if nx % 4 == 0 else 1), (2 if nx % 2 == 0 else 1)
    devices = lax.axis_size("gx")
    stages = (devices - 1).bit_length()
    crossed = lax.axis_size("gz") == 2
    full = lambda *lead: jax.ShapeDtypeStruct(lead + (ROWS, nz), F32)
    vec = lambda *lead: jax.ShapeDtypeStruct(lead + (nz,), F32)
    cost = lambda n: pl.CostEstimate(flops=n * cells * nz, bytes_accessed=n * cells * nz, transcendentals=0)
    inputs = (lower_face, density.reshape(cells, nz), momentum.reshape(2, cells, nz))
    inputs = [pltpu.with_memory_space_constraint(x, pltpu.HBM) for x in inputs]
    density, momentum, flux_y, flux_z, sums, small_b, small_a, coefs, scalars = pl.pallas_call(
        functools.partial(first_kernel, chunks),
        in_specs=[HBM] * 3,
        out_specs=[VMEM] * 9,
        out_shape=[
            vec(cells),
            vec(2, cells),
            vec(3 * nx * (ny + ROWS) + ROWS),
            vec(3 * cells),
            vec(12 * ny),
            vec(3 * ROWS),
            vec(3 * ROWS),
            full(2 * nx),
            full(),
        ],
        scratch_shapes=[pltpu.SMEM((nx,), F32), pltpu.SemaphoreType.DMA((1 + 2 * chunks,))],
        compiler_params=params(),
        name="load",
    )(*inputs)
    got_a, got_b = swap_edges(small_a, small_b, crossed)
    edge_a, edge_b = [
        pl.pallas_call(
            functools.partial(pack_kernel, nx, second),
            in_specs=[VMEM] * 2,
            out_specs=VMEM,
            out_shape=vec(9, nx),
            compiler_params=params(),
            cost_estimate=cost(PACK_COST),
            name="pack",
        )(density, momentum)
        for second in (False, True)
    ]
    far_a, far_b = swap_edges(edge_a, edge_b)
    sums_low, sums_high = swap_whole(sums, "gz")
    z_low, z_high = swap_whole(flux_z, "gz")
    rhs = pl.pallas_call(
        functools.partial(rhs_kernel, nx),
        in_specs=[VMEM] * 6,
        out_specs=VMEM,
        out_shape=vec(3, cells),
        compiler_params=params(),
        cost_estimate=cost(RHS_COST),
        name="rhs",
    )(density, momentum, flux_y, flux_z, z_low, z_high)
    halos = pl.pallas_call(
        halo_kernel,
        in_specs=[VMEM] * 2,
        out_specs=VMEM,
        out_shape=full(6, 2),
        compiler_params=params(),
        cost_estimate=cost(HALO_COST),
        name="halo",
    )(got_a, got_b)
    handled = (sums_low, sums, sums) if crossed else (sums, sums_low, sums_high)
    msg_shapes = [full(6 * tiles + 1), full(3 * tiles + 1)]
    own_shapes = [full(6 * tiles + 1), full(9 * tiles + 2)]
    msg, *own = pl.pallas_call(
        functools.partial(second_kernel, stages),
        in_specs=[VMEM] * 5,
        out_specs=[VMEM] * (1 + (stages == 1)),
        out_shape=[msg_shapes[1], own_shapes[1]] if stages == 1 else msg_shapes[:1],
        scratch_shapes=[pltpu.VMEM((6, ny + 2 * ROWS, nz), F32)],
        compiler_params=params(),
        cost_estimate=cost(FACE_COST),
        name="interface",
    )(halos, *handled, scalars)
    other = swap(msg, "gx", partner_by(devices, 1), crossed and stages == 1)
    for stage in range(stages - 1):
        closing_next = stage + 2 == stages
        msg, *own = pl.pallas_call(
            functools.partial(join_kernel, stage, stages, tiles),
            in_specs=[VMEM, VMEM, ANY] + [VMEM] * len(own),
            out_specs=[VMEM] * 2,
            out_shape=[msg_shapes[closing_next], own_shapes[closing_next]],
            compiler_params=params(),
            cost_estimate=cost(JOIN_COST),
            name="join",
        )(msg, other, rhs, *own)
        other = swap(msg, "gx", partner_by(devices, 2 << stage), crossed and closing_next)
    own = own[0]
    if crossed:
        own, _ = swap_whole(own, "gz")
    rhs = pl.pallas_call(
        functools.partial(edge_kernel, nx),
        in_specs=[VMEM] * 2,
        out_specs=VMEM,
        out_shape=vec(3, cells),
        input_output_aliases={0: 0},
        compiler_params=params(),
        cost_estimate=cost(EDGE_COST),
        name="edge",
    )(rhs, far_b)
    _, ahead, behind = pl.pallas_call(
        functools.partial(sums_kernel, nx),
        in_specs=[VMEM] * 3,
        out_specs=[VMEM] * 3,
        out_shape=[vec(3, cells)] + [full(3, nx, tiles)] * 2,
        input_output_aliases={0: 0},
        compiler_params=params(),
        cost_estimate=cost(SUMS_COST),
        name="sums",
    )(rhs, far_a, coefs)
    updated = pl.pallas_call(
        functools.partial(last_kernel, stages, parts),
        in_specs=[VMEM] * 6,
        out_specs=HBM,
        out_shape=full(3, nx, tiles),
        scratch_shapes=[
            pltpu.VMEM((3, nx, tiles, ROWS, nz), F32),
            pltpu.SemaphoreType.DMA((3 * parts,)),
        ],
        compiler_params=params(),
        name="solve",
    )(ahead, behind, coefs, scalars, other, own)
    return updated.reshape(3, nx, ny, nz)


def solution(mesh):
    placed = (P("gx", "gy", "gz"), P(None, "gx", "gy", "gz"), P("gx"))
    return jax.shard_map(
        on_device, mesh=mesh, in_specs=placed, out_specs=P(None, "gx", "gy", "gz"), check_vma=False
    )
```

```python
import functools

import jax
import jax.numpy as jnp
from jax import lax
from jax.experimental import pallas as pl
from jax.experimental.pallas import tpu as pltpu
from jax.sharding import PartitionSpec as P

time_step = 0.2
scale = time_step / 60.0
ROWS = 8
RHS_COST, SUMS_COST, JOIN_COST, EDGE_COST, FACE_COST, PACK_COST, HALO_COST = 60, 200, 20, 20000, 200000, 20000, 20
F32 = jnp.float32
VMEM = pl.BlockSpec(memory_space=pltpu.VMEM)
ANY = pl.BlockSpec(memory_space=pl.ANY)
HBM = pl.BlockSpec(memory_space=pltpu.HBM)


def pairing(count, odd):
    pairs = []
    for low in range(1 if odd else 0, count, 2):
        high = (low + 1) % count
        pairs += [(low, high), (high, low)]
    return pairs


def partner_by(count, step):
    return [(i, i ^ step) for i in range(count)]


def rows_of(block):
    return block.reshape(block.shape[0] * block.shape[1], block.shape[2])


def shifted_z(own, low, high, k):
    nz = own.shape[-1]
    if nz % 128 == 0:
        lane = lax.broadcasted_iota(jnp.int32, own.shape, own.ndim - 1)
        if k > 0:
            return pltpu.roll(jnp.where(lane < k, high, own), nz - k, own.ndim - 1)
        return pltpu.roll(jnp.where(lane >= nz + k, low, own), -k, own.ndim - 1)
    if k > 0:
        return jnp.concatenate([own[..., k:], high[..., :k]], -1)
    return jnp.concatenate([low[..., nz + k :], own[..., : nz + k]], -1)


def sixth(take):
    return 45.0 * (take(1) - take(-1)) - 9.0 * (take(2) - take(-2)) + (take(3) - take(-3))


def sixth_z(own, low, high):
    return sixth(lambda k: shifted_z(own, low, high, k))


def join(left, right):
    inv_delta = 1.0 / (right[5] + right[2] + left[3])
    jump = (right[0] - left[1]) * inv_delta
    from_in = left[4] * inv_delta
    from_out = right[4] * inv_delta
    group = (
        left[0] + left[4] * jump,
        right[1] - right[4] * jump,
        left[2] - left[4] * from_in,
        right[3] - right[4] * from_out,
        left[4] * from_out,
        left[5],
        right[6],
    )
    return group, (jump, from_in, from_out)


def pick(cond, yes, no):
    return tuple(jnp.where(cond, a, b) for a, b in zip(yes, no))


def join_own(is_left, own, other, forms):
    left = pick(is_left, own, other)
    right = pick(is_left, other, own)
    group, (jump, from_in, from_out) = join(left, right)
    new = []
    for c0, c1, c2 in forms:
        through = jnp.where(is_left, c2, c1)
        new.append(
            (
                c0 + through * jump,
                jnp.where(is_left, c1, 0.0) + through * from_in,
                jnp.where(is_left, 0.0, c2) + through * from_out,
            )
        )
    return group, new


def closing(is_left, group, forms):
    first, last, alpha, beta, m, inv_first, inv_last = group
    kappa = 1.0 / jnp.where(is_left, inv_first + alpha, inv_last + beta)
    outer = jnp.where(is_left, first, -last) * kappa
    gain = kappa * m
    facing = jnp.where(is_left, last - m * outer, first + m * outer)
    resist = jnp.where(is_left, beta, alpha + inv_first) - m * gain
    out = []
    for c0, c1, c2 in forms:
        far = jnp.where(is_left, c1, c2)
        near = jnp.where(is_left, c2, c1)
        out.append((c0 + far * outer, far * gain + near))
    return facing, resist, out


def put_scalars(ref, block, values):
    for row, value in enumerate(values):
        ref[block, row : row + 1] = value


def get_scalars(ref, block, count):
    return [ref[block, row : row + 1] for row in range(count)]


def store_group(ref, group, tiles):
    for f in range(3):
        ref[f * tiles : (f + 1) * tiles] = group[0][f]
        ref[(3 + f) * tiles : (4 + f) * tiles] = group[1][f]
    put_scalars(ref, 6 * tiles, group[2:])


def load_group(ref, tiles):
    shape = (3, tiles) + ref.shape[1:]
    first = ref[: 3 * tiles].reshape(shape)
    last = ref[3 * tiles : 6 * tiles].reshape(shape)
    return (first, last, *get_scalars(ref, 6 * tiles, 5))


def store_closing(msg_ref, own_ref, facing, resist, out, tiles):
    own_ref[6 * tiles + 1 : 9 * tiles + 1] = facing.reshape((3 * tiles,) + facing.shape[2:])
    put_scalars(own_ref, 9 * tiles + 1, [resist])
    for f in range(3):
        msg_ref[f * tiles : (f + 1) * tiles] = facing[f]
        own_ref[f * tiles : (f + 1) * tiles] = out[0][0][f]
        own_ref[(3 + f) * tiles : (4 + f) * tiles] = out[1][0][f]
    put_scalars(msg_ref, 3 * tiles, [resist])
    put_scalars(own_ref, 6 * tiles, [out[0][1], out[1][1]])


def store_forms(ref, forms, tiles):
    for f in range(3):
        ref[f * tiles : (f + 1) * tiles] = forms[0][0][f]
        ref[(3 + f) * tiles : (4 + f) * tiles] = forms[1][0][f]
    put_scalars(ref, 6 * tiles, [*forms[0][1:], *forms[1][1:]])


def load_forms(ref, tiles):
    shape = (3, tiles) + ref.shape[1:]
    scalars = get_scalars(ref, 6 * tiles, 4)
    return [
        (ref[: 3 * tiles].reshape(shape), scalars[0], scalars[1]),
        (ref[3 * tiles : 6 * tiles].reshape(shape), scalars[2], scalars[3]),
    ]


def sums_at(ny, side, k):
    start = (2 * k + side) * ny
    return slice(start, start + ny)


def pick_edges(ref_a, ref_b, take):
    odd = lax.rem(lax.axis_index("gy"), 2)
    for ref, high in ((ref_a, 1 - odd), (ref_b, odd)):
        take(ref, high)


def first_kernel(
    chunks, faces, density, momentum,
    rho_v, mom_v, flux_y, flux_z, sums, small_b, small_a, coefs, scalars,
    face_s, sems,
):
    nx = faces.shape[0]
    nz = density.shape[1]
    ny = density.shape[0] // nx
    tiles = ny // ROWS
    face_copy = pltpu.make_async_copy(faces, face_s, sems.at[0])
    face_copy.start()
    step = nx * ny // chunks
    copies = []
    for c in range(chunks):
        at = pl.ds(c * step, step)
        copies.append(
            (
                pltpu.make_async_copy(density.at[at], rho_v.at[at], sems.at[1 + 2 * c]),
                pltpu.make_async_copy(momentum.at[:, at], mom_v.at[:, at], sems.at[2 + 2 * c]),
            )
        )
        for copy in copies[-1]:
            copy.start()
    tile = (ROWS, nz)
    pitch = ny + ROWS
    for line in range(3 * nx + 1):
        flux_y[line * pitch : line * pitch + ROWS] = jnp.zeros(tile, F32)
    face_copy.wait()
    inv = [1.0 / jnp.full(tile, face_s[i], F32) for i in range(nx)]
    phi = [jnp.ones(tile, F32)]
    flux = phi[0]
    for i in range(1, nx):
        phi.append(phi[-1] + flux * inv[i])
        flux = flux + phi[-1]
    m = 1.0 / flux
    psi = [jnp.ones(tile, F32)]
    flux = psi[0]
    for i in range(nx - 1, 0, -1):
        psi.append(psi[-1] + flux * inv[i])
        flux = flux + psi[-1]
    psi = psi[::-1]
    for i in range(nx):
        coefs[i] = phi[i]
        coefs[nx + i] = psi[i] * m
    scalars[0:1] = (psi[0] * m)[0:1]
    scalars[1:2] = (phi[nx - 1] * m)[0:1]
    scalars[2:3] = m[0:1]
    scalars[3:4] = inv[0][0:1]
    scalars[4:5] = inv[nx - 1][0:1]
    scalars[5:8] = jnp.zeros((3, nz), F32)
    total = [[None] * 6, [None] * 6]
    for x in range(nx):
        if x % (nx // chunks) == 0:
            for copy in copies[x // (nx // chunks)]:
                copy.wait()
        at = slice(x * ny, (x + 1) * ny)
        rho, m0, m1 = [b.reshape(tiles, ROWS, nz) for b in (rho_v[at], mom_v[0, at], mom_v[1, at])]
        inv_rho = 1.0 / rho
        v0, v1 = m0 * inv_rho, m1 * inv_rho
        values = (m0, m0 * v0, m0 * v1, rho, m1, m1 * v1)
        for side, weight in enumerate((coefs[nx + x], coefs[x])):
            for k, value in enumerate(values):
                term = weight * value
                total[side][k] = term if x == 0 else total[side][k] + term
        for f in range(3):
            start = (f * nx + x) * pitch + ROWS
            flux_y[start : start + ny] = values[f].reshape(ny, nz)
            flux_z[f * nx * ny + x * ny : f * nx * ny + (x + 1) * ny] = values[(4, 2, 5)[f]].reshape(ny, nz)
    for side in range(2):
        for k in range(6):
            sums[sums_at(ny, side, k)] = total[side][k].reshape(ny, nz)

    def take_small(ref, high):
        sign = jnp.where(high == 1, scale, -scale)
        n1, n2, n3 = [
            sums[pl.ds(high * (ny - 1) + (1 - 2 * high) * k, 6, stride=ny)] * sign for k in range(3)
        ]
        ref[...] = jnp.zeros((3 * ROWS, nz), F32)
        ref[0:6] = 45.0 * n1 - 9.0 * n2 + n3
        ref[ROWS : ROWS + 6] = n2 - 9.0 * n1
        ref[2 * ROWS : 2 * ROWS + 6] = n1

    pick_edges(small_a, small_b, take_small)


def pack_kernel(nx, second, rho_v, mom_v, ref):
    ny = rho_v.shape[0] // (nx + 1)
    odd = lax.rem(lax.axis_index("gy"), 2)
    high = odd if second else 1 - odd
    sign = jnp.where(high == 1, scale, -scale)
    rows = [pl.ds(high * (ny - 1) + (1 - 2 * high) * k, nx, stride=ny) for k in range(3)]
    m0, m1, v0 = [], [], []
    for at in rows:
        m0.append(mom_v[0, at])
        m1.append(mom_v[1, at])
        v0.append(m0[-1] / rho_v[at] * sign)
    for f in range(3):
        n1, n2, n3 = [(m0[k] * sign, m0[k] * v0[k], m1[k] * v0[k])[f] for k in range(3)]
        ref[3 * f] = 45.0 * n1 - 9.0 * n2 + n3
        ref[3 * f + 1] = n2 - 9.0 * n1
        ref[3 * f + 2] = n1


def halos_y(is_odd, from_a, from_b):
    low = jnp.where(is_odd, from_a, from_b)
    high = jnp.where(is_odd, from_b, from_a)
    return low, high


def inner_kernel(sums, sums_low, sums_high, inner, pad):
    nz = sums.shape[1]
    ny = sums.shape[0] // 12
    pad[0:ROWS] = jnp.zeros((ROWS, nz), F32)
    pad[ROWS + ny : 2 * ROWS + ny] = jnp.zeros((ROWS, nz), F32)
    for side in range(2):
        for f, (state, along_y, along_z) in enumerate(((3, 0, 4), (0, 1, 2), (4, 2, 5))):
            pad[ROWS : ROWS + ny] = sums[sums_at(ny, side, along_y)]
            dy = sixth(lambda s: pad[ROWS + s : ROWS + s + ny])
            dz = sixth_z(*[r[sums_at(ny, side, along_z)] for r in (sums, sums_low, sums_high)])
            inner[sums_at(ny, side, f)] = sums[sums_at(ny, side, state)] - scale * (dy + dz)


def second_kernel(stages, small_a, small_b, inner, scalars, *refs):
    ny, nz = inner.shape[0] // 6, inner.shape[1]
    tiles = ny // ROWS
    block = refs[-1]
    is_odd = lax.rem(lax.axis_index("gy"), 2) == 1
    low, high = halos_y(is_odd, small_a[...], small_b[...])
    alpha, beta, m, inv_first, inv_last = [scalars[i : i + 1] for i in range(5)]
    block[0 : 6 * ny] = inner[...]
    for k in range(3):
        for row, edge in ((k, low), (ny - 1 - k, high)):
            at = pl.ds(row, 6, stride=ny)
            block[at] = block[at] + edge[k * ROWS : k * ROWS + 6]
    values = [block[sums_at(ny, side, f)].reshape(tiles, ROWS, nz) for side in range(2) for f in range(3)]
    first = jnp.stack(values[:3])
    last = jnp.stack(values[3:]) * m
    group = (first, last, alpha, beta, m, inv_first, inv_last)
    if stages == 1:
        is_left = lax.rem(lax.axis_index("gx"), 2) == 0
        zero = jnp.zeros_like(first)
        one = jnp.ones_like(alpha)
        forms = [(zero, one, 0.0 * one), (zero, 0.0 * one, one)]
        facing, resist, out = closing(is_left, group, forms)
        store_closing(refs[0], refs[1], facing, resist, out, tiles)
    else:
        store_group(refs[0], group, tiles)


def join_kernel(stage, stages, tiles, *refs):
    refs = refs[:2] + refs[3:]
    if stage == 0:
        mine, other, msg, own = refs
        shape = (3, tiles) + mine.shape[1:]
        zero, one = jnp.zeros(shape, F32), jnp.ones((1, shape[-1]), F32)
        forms = [(zero, one, 0.0 * one), (zero, 0.0 * one, one)]
    else:
        mine, other, forms_ref, msg, own = refs
        forms = load_forms(forms_ref, tiles)
    at = lax.axis_index("gx")
    is_left = lax.rem(lax.div(at, 1 << stage), 2) == 0
    group, forms = join_own(is_left, load_group(mine, tiles), load_group(other, tiles), forms)
    if stage + 2 == stages:
        is_left = lax.rem(lax.div(at, 2 << stage), 2) == 0
        facing, resist, out = closing(is_left, group, forms)
        store_closing(msg, own, facing, resist, out, tiles)
    else:
        store_group(msg, group, tiles)
        store_forms(own, forms, tiles)


def rhs_kernel(nx, density, momentum, flux_y, flux_z, flux_z_low, flux_z_high, rhs):
    ny = density.shape[0] // (nx + 1)
    pitch = ny + ROWS
    for f in range(3):
        for x in range(nx):
            at = (f * nx + x) * pitch + ROWS
            dy = sixth(lambda s: flux_y[at + s : at + s + ny])
            cells = slice(x * ny, (x + 1) * ny)
            lines = slice((f * nx + x) * ny, (f * nx + x + 1) * ny)
            dz = sixth_z(*[r[lines] for r in (flux_z, flux_z_low, flux_z_high)])
            state = density[cells] if f == 0 else momentum[f - 1, cells]
            rhs[f, cells] = state - scale * (dy + dz)


def add_edge(nx, rhs, edge, high):
    ny = rhs.shape[1] // (nx + 1)
    for f in range(3):
        for k in range(3):
            at = pl.ds(high * (ny - 1) + (1 - 2 * high) * k, nx, stride=ny)
            rhs[f, at] = rhs[f, at] + edge[3 * f + k]


def edge_kernel(nx, rhs_in, edge_b, rhs):
    add_edge(nx, rhs, edge_b, lax.rem(lax.axis_index("gy"), 2))


def sums_kernel(nx, rhs_in, edge_a, coefs, rhs, ahead, behind):
    ny, nz = rhs.shape[1] // (nx + 1), rhs.shape[2]
    shape = (ny // ROWS, ROWS, nz)
    add_edge(nx, rhs, edge_a, 1 - lax.rem(lax.axis_index("gy"), 2))
    for f in range(3):
        total = None
        for x in range(nx):
            r = rhs[f, x * ny : (x + 1) * ny].reshape(shape)
            total = coefs[x] * r if x == 0 else total + coefs[x] * r
            ahead[f, x] = total
        total = jnp.zeros(shape, F32)
        for x in range(nx - 1, -1, -1):
            behind[f, x] = total
            if x > 0:
                r = rhs[f, x * ny : (x + 1) * ny].reshape(shape)
                total = total + coefs[nx + x] * r


def last_kernel(stages, parts, ahead, behind, coefs, scalars, other, own, updated, out_v, sems):
    _, nx, tiles, _, nz = ahead.shape
    is_left = lax.rem(lax.div(lax.axis_index("gx"), 1 << (stages - 1)), 2) == 0
    sign = jnp.where(is_left, 1.0, -1.0)
    inv = sign / (own[9 * tiles + 1, 0:1] + other[3 * tiles, 0:1])
    m = scalars[2:3]
    copies = []
    for f in range(3):
        at = slice(f * tiles, (f + 1) * tiles)
        mid = (other[at] - own[(6 + f) * tiles + 1 : (7 + f) * tiles + 1]) * inv
        jin = own[at] + own[6 * tiles, 0:1] * mid
        jout = m * (own[(3 + f) * tiles : (4 + f) * tiles] + own[6 * tiles, 1:2] * mid)
        for x in range(nx):
            out_v[f, x] = coefs[nx + x] * (ahead[f, x] - jin) + coefs[x] * (behind[f, x] + jout)
            if (x + 1) % (nx // parts) == 0:
                part = pl.ds(x + 1 - nx // parts, nx // parts)
                copy = pltpu.make_async_copy(out_v.at[f, part], updated.at[f, part], sems.at[len(copies)])
                copy.start()
                copies.append(copy)
    for copy in copies:
        copy.wait()


def params(limit=48):
    return pltpu.CompilerParams(vmem_limit_bytes=limit * 1024 * 1024)


def swap(block, axis, pairs, crossed):
    if not crossed:
        return lax.ppermute(block, axis, pairs)
    both = [(2 * a + c, 2 * b + 1 - c) for a, b in pairs for c in range(2)]
    return lax.ppermute(block, (axis, "gz"), both)


def swap_edges(block_a, block_b, crossed=False):
    count = lax.axis_size("gy")
    return (
        swap(block_a, "gy", pairing(count, False), crossed),
        swap(block_b, "gy", pairing(count, True), crossed),
    )


def swap_whole(block, axis):
    count = lax.axis_size(axis)
    if count == 2:
        got = lax.ppermute(block, axis, pairing(2, False))
        return got, got
    ring = [(i, (i + 1) % count) for i in range(count)]
    return lax.ppermute(block, axis, ring), lax.ppermute(block, axis, [(b, a) for a, b in ring])


def on_device(density, momentum, lower_face):
    nx, ny, nz = density.shape
    tiles = ny // ROWS
    cells = nx * ny
    chunks, parts = (4 if nx % 4 == 0 else 1), (2 if nx % 2 == 0 else 1)
    devices = lax.axis_size("gx")
    stages = (devices - 1).bit_length()
    crossed = lax.axis_size("gz") == 2
    full = lambda *lead: jax.ShapeDtypeStruct(lead + (ROWS, nz), F32)
    vec = lambda *lead: jax.ShapeDtypeStruct(lead + (nz,), F32)
    cost = lambda n: pl.CostEstimate(flops=n * cells * nz, bytes_accessed=n * cells * nz, transcendentals=0)
    inputs = (lower_face, density.reshape(cells, nz), momentum.reshape(2, cells, nz))
    inputs = [pltpu.with_memory_space_constraint(x, pltpu.HBM) for x in inputs]
    density, momentum, flux_y, flux_z, sums, small_b, small_a, coefs, scalars = pl.pallas_call(
        functools.partial(first_kernel, chunks),
        in_specs=[HBM] * 3,
        out_specs=[VMEM] * 9,
        out_shape=[
            vec(cells + ny),
            vec(2, cells + ny),
            vec(3 * nx * (ny + ROWS) + ROWS),
            vec(3 * cells),
            vec(12 * ny),
            vec(3 * ROWS),
            vec(3 * ROWS),
            full(2 * nx),
            full(),
        ],
        scratch_shapes=[pltpu.SMEM((nx,), F32), pltpu.SemaphoreType.DMA((1 + 2 * chunks,))],
        compiler_params=params(),
        name="load",
    )(*inputs)
    got_a, got_b = swap_edges(small_a, small_b, crossed)
    edge_a, edge_b = [
        pl.pallas_call(
            functools.partial(pack_kernel, nx, second),
            in_specs=[VMEM] * 2,
            out_specs=VMEM,
            out_shape=vec(9, nx),
            compiler_params=params(),
            cost_estimate=cost(PACK_COST),
            name="pack",
        )(density, momentum)
        for second in (False, True)
    ]
    far_a, far_b = swap_edges(edge_a, edge_b)
    sums_low, sums_high = swap_whole(sums, "gz")
    z_low, z_high = swap_whole(flux_z, "gz")
    rhs = pl.pallas_call(
        functools.partial(rhs_kernel, nx),
        in_specs=[VMEM] * 6,
        out_specs=VMEM,
        out_shape=vec(3, cells + ny),
        compiler_params=params(),
        cost_estimate=cost(RHS_COST),
        name="rhs",
    )(density, momentum, flux_y, flux_z, z_low, z_high)
    handled = (sums_low, sums, sums) if crossed else (sums, sums_low, sums_high)
    inner = pl.pallas_call(
        inner_kernel,
        in_specs=[VMEM] * 3,
        out_specs=VMEM,
        out_shape=vec(6 * ny),
        scratch_shapes=[pltpu.VMEM((ny + 2 * ROWS, nz), F32)],
        compiler_params=params(),
        cost_estimate=cost(HALO_COST),
        name="inner",
    )(*handled)
    msg_shapes = [full(6 * tiles + 1), full(3 * tiles + 1)]
    own_shapes = [full(6 * tiles + 1), full(9 * tiles + 2)]
    msg, *own = pl.pallas_call(
        functools.partial(second_kernel, stages),
        in_specs=[VMEM] * 4,
        out_specs=[VMEM] * (1 + (stages == 1)),
        out_shape=[msg_shapes[1], own_shapes[1]] if stages == 1 else msg_shapes[:1],
        scratch_shapes=[pltpu.VMEM((7 * ny, nz), F32)],
        compiler_params=params(),
        cost_estimate=cost(FACE_COST),
        name="interface",
    )(got_a, got_b, inner, scalars)
    other = swap(msg, "gx", partner_by(devices, 1), crossed and stages == 1)
    for stage in range(stages - 1):
        closing_next = stage + 2 == stages
        msg, *own = pl.pallas_call(
            functools.partial(join_kernel, stage, stages, tiles),
            in_specs=[VMEM, VMEM, ANY] + [VMEM] * len(own),
            out_specs=[VMEM] * 2,
            out_shape=[msg_shapes[closing_next], own_shapes[closing_next]],
            compiler_params=params(),
            cost_estimate=cost(JOIN_COST),
            name="join",
        )(msg, other, rhs, *own)
        other = swap(msg, "gx", partner_by(devices, 2 << stage), crossed and closing_next)
    own = own[0]
    if crossed:
        own, _ = swap_whole(own, "gz")
    rhs = pl.pallas_call(
        functools.partial(edge_kernel, nx),
        in_specs=[VMEM] * 2,
        out_specs=VMEM,
        out_shape=vec(3, cells + ny),
        input_output_aliases={0: 0},
        compiler_params=params(),
        cost_estimate=cost(EDGE_COST),
        name="edge",
    )(rhs, far_b)
    _, ahead, behind = pl.pallas_call(
        functools.partial(sums_kernel, nx),
        in_specs=[VMEM] * 3,
        out_specs=[VMEM] * 3,
        out_shape=[vec(3, cells + ny)] + [full(3, nx, tiles)] * 2,
        input_output_aliases={0: 0},
        compiler_params=params(),
        cost_estimate=cost(SUMS_COST),
        name="sums",
    )(rhs, far_a, coefs)
    updated = pl.pallas_call(
        functools.partial(last_kernel, stages, parts),
        in_specs=[VMEM] * 6,
        out_specs=HBM,
        out_shape=full(3, nx, tiles),
        scratch_shapes=[
            pltpu.VMEM((3, nx, tiles, ROWS, nz), F32),
            pltpu.SemaphoreType.DMA((3 * parts,)),
        ],
        compiler_params=params(),
        name="solve",
    )(ahead, behind, coefs, scalars, other, own)
    return updated.reshape(3, nx, ny, nz)


def solution(mesh):
    placed = (P("gx", "gy", "gz"), P(None, "gx", "gy", "gz"), P("gx"))
    return jax.shard_map(
        on_device, mesh=mesh, in_specs=placed, out_specs=P(None, "gx", "gy", "gz"), check_vma=False
    )
```

```python
import functools

import jax
import jax.numpy as jnp
from jax import lax
from jax.experimental import pallas as pl
from jax.experimental.pallas import tpu as pltpu
from jax.sharding import PartitionSpec as P

time_step = 0.2
scale = time_step / 60.0
ROWS = 8
RHS_COST, SUMS_COST, JOIN_COST, EDGE_COST, FACE_COST, PACK_COST, HALO_COST = 60, 200, 20, 20000, 200000, 20000, 20
F32 = jnp.float32
VMEM = pl.BlockSpec(memory_space=pltpu.VMEM)
ANY = pl.BlockSpec(memory_space=pl.ANY)
HBM = pl.BlockSpec(memory_space=pltpu.HBM)


def pairing(count, odd):
    pairs = []
    for low in range(1 if odd else 0, count, 2):
        high = (low + 1) % count
        pairs += [(low, high), (high, low)]
    return pairs


def partner_by(count, step):
    return [(i, i ^ step) for i in range(count)]


def shifted_z(own, low, high, k):
    nz = own.shape[-1]
    if nz % 128 == 0:
        lane = lax.broadcasted_iota(jnp.int32, own.shape, own.ndim - 1)
        if k > 0:
            return pltpu.roll(jnp.where(lane < k, high, own), nz - k, own.ndim - 1)
        return pltpu.roll(jnp.where(lane >= nz + k, low, own), -k, own.ndim - 1)
    if k > 0:
        return jnp.concatenate([own[..., k:], high[..., :k]], -1)
    return jnp.concatenate([low[..., nz + k :], own[..., : nz + k]], -1)


def sixth(take):
    return 45.0 * (take(1) - take(-1)) - 9.0 * (take(2) - take(-2)) + (take(3) - take(-3))


def sixth_z(own, low, high):
    return sixth(lambda k: shifted_z(own, low, high, k))


def join(left, right):
    inv_delta = 1.0 / (right[5] + right[2] + left[3])
    jump = (right[0] - left[1]) * inv_delta
    from_in = left[4] * inv_delta
    from_out = right[4] * inv_delta
    group = (
        left[0] + left[4] * jump,
        right[1] - right[4] * jump,
        left[2] - left[4] * from_in,
        right[3] - right[4] * from_out,
        left[4] * from_out,
        left[5],
        right[6],
    )
    return group, (jump, from_in, from_out)


def pick(cond, yes, no):
    return tuple(jnp.where(cond, a, b) for a, b in zip(yes, no))


def join_own(is_left, own, other, forms):
    left = pick(is_left, own, other)
    right = pick(is_left, other, own)
    group, (jump, from_in, from_out) = join(left, right)
    new = []
    for c0, c1, c2 in forms:
        through = jnp.where(is_left, c2, c1)
        new.append(
            (
                c0 + through * jump,
                jnp.where(is_left, c1, 0.0) + through * from_in,
                jnp.where(is_left, 0.0, c2) + through * from_out,
            )
        )
    return group, new


def closing(is_left, group, forms):
    first, last, alpha, beta, m, inv_first, inv_last = group
    kappa = 1.0 / jnp.where(is_left, inv_first + alpha, inv_last + beta)
    outer = jnp.where(is_left, first, -last) * kappa
    gain = kappa * m
    facing = jnp.where(is_left, last - m * outer, first + m * outer)
    resist = jnp.where(is_left, beta, alpha + inv_first) - m * gain
    out = []
    for c0, c1, c2 in forms:
        far = jnp.where(is_left, c1, c2)
        near = jnp.where(is_left, c2, c1)
        out.append((c0 + far * outer, far * gain + near))
    return facing, resist, out


def put_scalars(ref, block, values):
    for row, value in enumerate(values):
        ref[block, row : row + 1] = value


def get_scalars(ref, block, count):
    return [ref[block, row : row + 1] for row in range(count)]


def store_group(ref, group, tiles):
    for f in range(3):
        ref[f * tiles : (f + 1) * tiles] = group[0][f]
        ref[(3 + f) * tiles : (4 + f) * tiles] = group[1][f]
    put_scalars(ref, 6 * tiles, group[2:])


def load_group(ref, tiles):
    shape = (3, tiles) + ref.shape[1:]
    first = ref[: 3 * tiles].reshape(shape)
    last = ref[3 * tiles : 6 * tiles].reshape(shape)
    return (first, last, *get_scalars(ref, 6 * tiles, 5))


def store_closing(msg_ref, own_ref, facing, resist, out, tiles):
    own_ref[6 * tiles + 1 : 9 * tiles + 1] = facing.reshape((3 * tiles,) + facing.shape[2:])
    put_scalars(own_ref, 9 * tiles + 1, [resist])
    for f in range(3):
        msg_ref[f * tiles : (f + 1) * tiles] = facing[f]
        own_ref[f * tiles : (f + 1) * tiles] = out[0][0][f]
        own_ref[(3 + f) * tiles : (4 + f) * tiles] = out[1][0][f]
    put_scalars(msg_ref, 3 * tiles, [resist])
    put_scalars(own_ref, 6 * tiles, [out[0][1], out[1][1]])


def store_forms(ref, forms, tiles):
    for f in range(3):
        ref[f * tiles : (f + 1) * tiles] = forms[0][0][f]
        ref[(3 + f) * tiles : (4 + f) * tiles] = forms[1][0][f]
    put_scalars(ref, 6 * tiles, [*forms[0][1:], *forms[1][1:]])


def load_forms(ref, tiles):
    shape = (3, tiles) + ref.shape[1:]
    scalars = get_scalars(ref, 6 * tiles, 4)
    return [
        (ref[: 3 * tiles].reshape(shape), scalars[0], scalars[1]),
        (ref[3 * tiles : 6 * tiles].reshape(shape), scalars[2], scalars[3]),
    ]


def sums_at(ny, side, k):
    start = (2 * k + side) * ny
    return slice(start, start + ny)


def pick_edges(ref_a, ref_b, take):
    odd = lax.rem(lax.axis_index("gy"), 2)
    for ref, high in ((ref_a, 1 - odd), (ref_b, odd)):
        take(ref, high)


def first_kernel(
    chunks, faces, density, momentum,
    rho_v, mom_v, flux_y, flux_z, sums, small_b, small_a, coefs, scalars,
    face_s, sems,
):
    nx = faces.shape[0]
    nz = density.shape[1]
    ny = density.shape[0] // nx
    tiles = ny // ROWS
    face_copy = pltpu.make_async_copy(faces, face_s, sems.at[0])
    face_copy.start()
    step = nx * ny // chunks
    copies = []
    for c in range(chunks):
        at = pl.ds(c * step, step)
        copies.append(
            (
                pltpu.make_async_copy(density.at[at], rho_v.at[at], sems.at[1 + 2 * c]),
                pltpu.make_async_copy(momentum.at[:, at], mom_v.at[:, at], sems.at[2 + 2 * c]),
            )
        )
        for copy in copies[-1]:
            copy.start()
    tile = (ROWS, nz)
    pitch = ny + ROWS
    for line in range(3 * nx + 1):
        flux_y[line * pitch : line * pitch + ROWS] = jnp.zeros(tile, F32)
    face_copy.wait()
    inv = [1.0 / jnp.full(tile, face_s[i], F32) for i in range(nx)]
    phi = [jnp.ones(tile, F32)]
    flux = phi[0]
    for i in range(1, nx):
        phi.append(phi[-1] + flux * inv[i])
        flux = flux + phi[-1]
    m = 1.0 / flux
    psi = [jnp.ones(tile, F32)]
    flux = psi[0]
    for i in range(nx - 1, 0, -1):
        psi.append(psi[-1] + flux * inv[i])
        flux = flux + psi[-1]
    psi = psi[::-1]
    for i in range(nx):
        coefs[i] = phi[i]
        coefs[nx + i] = psi[i] * m
    scalars[0:1] = (psi[0] * m)[0:1]
    scalars[1:2] = (phi[nx - 1] * m)[0:1]
    scalars[2:3] = m[0:1]
    scalars[3:4] = inv[0][0:1]
    scalars[4:5] = inv[nx - 1][0:1]
    scalars[5:8] = jnp.zeros((3, nz), F32)
    total = [[None] * 6, [None] * 6]
    for x in range(nx):
        if x % (nx // chunks) == 0:
            for copy in copies[x // (nx // chunks)]:
                copy.wait()
        at = slice(x * ny, (x + 1) * ny)
        rho, m0, m1 = [b.reshape(tiles, ROWS, nz) for b in (rho_v[at], mom_v[0, at], mom_v[1, at])]
        inv_rho = 1.0 / rho
        v0, v1 = m0 * inv_rho, m1 * inv_rho
        values = (m0, m0 * v0, m0 * v1, rho, m1, m1 * v1)
        for side, weight in enumerate((coefs[nx + x], coefs[x])):
            for k, value in enumerate(values):
                term = weight * value
                total[side][k] = term if x == 0 else total[side][k] + term
        for f in range(3):
            start = (f * nx + x) * pitch + ROWS
            flux_y[start : start + ny] = values[f].reshape(ny, nz)
            flux_z[f * nx * ny + x * ny : f * nx * ny + (x + 1) * ny] = values[(4, 2, 5)[f]].reshape(ny, nz)
    for side in range(2):
        for k in range(6):
            sums[sums_at(ny, side, k)] = total[side][k].reshape(ny, nz)

    def take_small(ref, high):
        sign = jnp.where(high == 1, scale, -scale)
        n1, n2, n3 = [
            sums[pl.ds(high * (ny - 1) + (1 - 2 * high) * k, 6, stride=ny)] * sign for k in range(3)
        ]
        ref[...] = jnp.zeros((3 * ROWS, nz), F32)
        ref[0:6] = 45.0 * n1 - 9.0 * n2 + n3
        ref[ROWS : ROWS + 6] = n2 - 9.0 * n1
        ref[2 * ROWS : 2 * ROWS + 6] = n1

    pick_edges(small_a, small_b, take_small)


def pack_kernel(nx, second, rho_v, mom_v, ref):
    ny = rho_v.shape[0] // (nx + 1)
    odd = lax.rem(lax.axis_index("gy"), 2)
    high = odd if second else 1 - odd
    sign = jnp.where(high == 1, scale, -scale)
    rows = [pl.ds(high * (ny - 1) + (1 - 2 * high) * k, nx, stride=ny) for k in range(3)]
    m0, m1, v0 = [], [], []
    for at in rows:
        m0.append(mom_v[0, at])
        m1.append(mom_v[1, at])
        v0.append(m0[-1] / rho_v[at] * sign)
    for f in range(3):
        n1, n2, n3 = [(m0[k] * sign, m0[k] * v0[k], m1[k] * v0[k])[f] for k in range(3)]
        ref[3 * f] = 45.0 * n1 - 9.0 * n2 + n3
        ref[3 * f + 1] = n2 - 9.0 * n1
        ref[3 * f + 2] = n1


def halos_y(is_odd, from_a, from_b):
    low = jnp.where(is_odd, from_a, from_b)
    high = jnp.where(is_odd, from_b, from_a)
    return low, high


def inner_kernel(sums, sums_low, sums_high, inner, pad):
    nz = sums.shape[1]
    ny = sums.shape[0] // 12
    pad[0:ROWS] = jnp.zeros((ROWS, nz), F32)
    pad[ROWS + ny : 2 * ROWS + ny] = jnp.zeros((ROWS, nz), F32)
    for side in range(2):
        for f, (state, along_y, along_z) in enumerate(((3, 0, 4), (0, 1, 2), (4, 2, 5))):
            pad[ROWS : ROWS + ny] = sums[sums_at(ny, side, along_y)]
            dy = sixth(lambda s: pad[ROWS + s : ROWS + s + ny])
            dz = sixth_z(*[r[sums_at(ny, side, along_z)] for r in (sums, sums_low, sums_high)])
            inner[sums_at(ny, side, f)] = sums[sums_at(ny, side, state)] - scale * (dy + dz)


def second_kernel(stages, small_a, small_b, inner, scalars, *refs):
    ny, nz = inner.shape[0] // 6, inner.shape[1]
    tiles = ny // ROWS
    block = refs[-1]
    is_odd = lax.rem(lax.axis_index("gy"), 2) == 1
    low, high = halos_y(is_odd, small_a[...], small_b[...])
    alpha, beta, m, inv_first, inv_last = [scalars[i : i + 1] for i in range(5)]
    block[0 : 6 * ny] = inner[...]
    for k in range(3):
        for row, edge in ((k, low), (ny - 1 - k, high)):
            at = pl.ds(row, 6, stride=ny)
            block[at] = block[at] + edge[k * ROWS : k * ROWS + 6]
    values = [block[sums_at(ny, side, f)].reshape(tiles, ROWS, nz) for side in range(2) for f in range(3)]
    first = jnp.stack(values[:3])
    last = jnp.stack(values[3:]) * m
    group = (first, last, alpha, beta, m, inv_first, inv_last)
    if stages == 1:
        is_left = lax.rem(lax.axis_index("gx"), 2) == 0
        zero = jnp.zeros_like(first)
        one = jnp.ones_like(alpha)
        forms = [(zero, one, 0.0 * one), (zero, 0.0 * one, one)]
        facing, resist, out = closing(is_left, group, forms)
        store_closing(refs[0], refs[1], facing, resist, out, tiles)
    else:
        store_group(refs[0], group, tiles)


def join_kernel(stage, stages, tiles, *refs):
    refs = refs[:2] + refs[3:]
    if stage == 0:
        mine, other, msg, own = refs
        shape = (3, tiles) + mine.shape[1:]
        zero, one = jnp.zeros(shape, F32), jnp.ones((1, shape[-1]), F32)
        forms = [(zero, one, 0.0 * one), (zero, 0.0 * one, one)]
    else:
        mine, other, forms_ref, msg, own = refs
        forms = load_forms(forms_ref, tiles)
    at = lax.axis_index("gx")
    is_left = lax.rem(lax.div(at, 1 << stage), 2) == 0
    group, forms = join_own(is_left, load_group(mine, tiles), load_group(other, tiles), forms)
    if stage + 2 == stages:
        is_left = lax.rem(lax.div(at, 2 << stage), 2) == 0
        facing, resist, out = closing(is_left, group, forms)
        store_closing(msg, own, facing, resist, out, tiles)
    else:
        store_group(msg, group, tiles)
        store_forms(own, forms, tiles)


def rhs_kernel(nx, density, momentum, flux_y, flux_z, flux_z_low, flux_z_high, rhs):
    ny = density.shape[0] // (nx + 1)
    pitch = ny + ROWS
    for f in range(3):
        for x in range(nx):
            at = (f * nx + x) * pitch + ROWS
            dy = sixth(lambda s: flux_y[at + s : at + s + ny])
            cells = slice(x * ny, (x + 1) * ny)
            lines = slice((f * nx + x) * ny, (f * nx + x + 1) * ny)
            dz = sixth_z(*[r[lines] for r in (flux_z, flux_z_low, flux_z_high)])
            state = density[cells] if f == 0 else momentum[f - 1, cells]
            rhs[f, cells] = state - scale * (dy + dz)


def add_edge(nx, rhs, edge, high):
    ny = rhs.shape[1] // (nx + 1)
    for f in range(3):
        for k in range(3):
            at = pl.ds(high * (ny - 1) + (1 - 2 * high) * k, nx, stride=ny)
            rhs[f, at] = rhs[f, at] + edge[3 * f + k]


def edge_kernel(nx, rhs_in, edge_b, rhs):
    rhs[...] = rhs_in[...]
    add_edge(nx, rhs, edge_b, lax.rem(lax.axis_index("gy"), 2))


def sums_kernel(nx, rhs_in, edge_a, coefs, rhs, ahead, behind):
    ny, nz = rhs.shape[1] // (nx + 1), rhs.shape[2]
    shape = (ny // ROWS, ROWS, nz)
    rhs[...] = rhs_in[...]
    add_edge(nx, rhs, edge_a, 1 - lax.rem(lax.axis_index("gy"), 2))
    for f in range(3):
        total = None
        for x in range(nx):
            r = rhs[f, x * ny : (x + 1) * ny].reshape(shape)
            total = coefs[x] * r if x == 0 else total + coefs[x] * r
            ahead[f, x] = total
        total = jnp.zeros(shape, F32)
        for x in range(nx - 1, -1, -1):
            behind[f, x] = total
            if x > 0:
                r = rhs[f, x * ny : (x + 1) * ny].reshape(shape)
                total = total + coefs[nx + x] * r


def last_kernel(stages, parts, ahead, behind, coefs, scalars, other, own, updated, out_v, sems):
    _, nx, tiles, _, nz = ahead.shape
    is_left = lax.rem(lax.div(lax.axis_index("gx"), 1 << (stages - 1)), 2) == 0
    sign = jnp.where(is_left, 1.0, -1.0)
    inv = sign / (own[9 * tiles + 1, 0:1] + other[3 * tiles, 0:1])
    m = scalars[2:3]
    copies = []
    for f in range(3):
        at = slice(f * tiles, (f + 1) * tiles)
        mid = (other[at] - own[(6 + f) * tiles + 1 : (7 + f) * tiles + 1]) * inv
        jin = own[at] + own[6 * tiles, 0:1] * mid
        jout = m * (own[(3 + f) * tiles : (4 + f) * tiles] + own[6 * tiles, 1:2] * mid)
        for x in range(nx):
            out_v[f, x] = coefs[nx + x] * (ahead[f, x] - jin) + coefs[x] * (behind[f, x] + jout)
            if (x + 1) % (nx // parts) == 0:
                part = pl.ds(x + 1 - nx // parts, nx // parts)
                copy = pltpu.make_async_copy(out_v.at[f, part], updated.at[f, part], sems.at[len(copies)])
                copy.start()
                copies.append(copy)
    for copy in copies:
        copy.wait()


def params(limit=48):
    return pltpu.CompilerParams(vmem_limit_bytes=limit * 1024 * 1024)


def swap(block, axis, pairs, crossed):
    if not crossed:
        return lax.ppermute(block, axis, pairs)
    both = [(2 * a + c, 2 * b + 1 - c) for a, b in pairs for c in range(2)]
    return lax.ppermute(block, (axis, "gz"), both)


def swap_edges(block_a, block_b, crossed=False):
    count = lax.axis_size("gy")
    return (
        swap(block_a, "gy", pairing(count, False), crossed),
        swap(block_b, "gy", pairing(count, True), crossed),
    )


def swap_whole(block, axis):
    count = lax.axis_size(axis)
    if count == 2:
        got = lax.ppermute(block, axis, pairing(2, False))
        return got, got
    ring = [(i, (i + 1) % count) for i in range(count)]
    return lax.ppermute(block, axis, ring), lax.ppermute(block, axis, [(b, a) for a, b in ring])


def on_device(density, momentum, lower_face):
    nx, ny, nz = density.shape
    tiles = ny // ROWS
    cells = nx * ny
    chunks, parts = (4 if nx % 4 == 0 else 1), (2 if nx % 2 == 0 else 1)
    devices = lax.axis_size("gx")
    stages = (devices - 1).bit_length()
    crossed = lax.axis_size("gz") == 2
    full = lambda *lead: jax.ShapeDtypeStruct(lead + (ROWS, nz), F32)
    vec = lambda *lead: jax.ShapeDtypeStruct(lead + (nz,), F32)
    cost = lambda n: pl.CostEstimate(flops=n * cells * nz, bytes_accessed=n * cells * nz, transcendentals=0)
    inputs = (lower_face, density.reshape(cells, nz), momentum.reshape(2, cells, nz))
    inputs = [pltpu.with_memory_space_constraint(x, pltpu.HBM) for x in inputs]
    density, momentum, flux_y, flux_z, sums, small_b, small_a, coefs, scalars = pl.pallas_call(
        functools.partial(first_kernel, chunks),
        in_specs=[HBM] * 3,
        out_specs=[VMEM] * 9,
        out_shape=[
            vec(cells + ny),
            vec(2, cells + ny),
            vec(3 * nx * (ny + ROWS) + ROWS),
            vec(3 * cells),
            vec(12 * ny),
            vec(3 * ROWS),
            vec(3 * ROWS),
            full(2 * nx),
            full(),
        ],
        scratch_shapes=[pltpu.SMEM((nx,), F32), pltpu.SemaphoreType.DMA((1 + 2 * chunks,))],
        compiler_params=params(),
        name="load",
    )(*inputs)
    got_a, got_b = swap_edges(small_a, small_b, crossed)
    edge_a, edge_b = [
        pl.pallas_call(
            functools.partial(pack_kernel, nx, second),
            in_specs=[VMEM] * 2,
            out_specs=VMEM,
            out_shape=vec(9, nx),
            compiler_params=params(),
            cost_estimate=cost(PACK_COST),
            name="pack",
        )(density, momentum)
        for second in (False, True)
    ]
    far_a, far_b = swap_edges(edge_a, edge_b)
    sums_low, sums_high = swap_whole(sums, "gz")
    z_low, z_high = swap_whole(flux_z, "gz")
    rhs = pl.pallas_call(
        functools.partial(rhs_kernel, nx),
        in_specs=[VMEM] * 6,
        out_specs=VMEM,
        out_shape=vec(3, cells + ny),
        compiler_params=params(),
        cost_estimate=cost(RHS_COST),
        name="rhs",
    )(density, momentum, flux_y, flux_z, z_low, z_high)
    handled = (sums_low, sums, sums) if crossed else (sums, sums_low, sums_high)
    inner = pl.pallas_call(
        inner_kernel,
        in_specs=[VMEM] * 3,
        out_specs=VMEM,
        out_shape=vec(6 * ny),
        scratch_shapes=[pltpu.VMEM((ny + 2 * ROWS, nz), F32)],
        compiler_params=params(),
        cost_estimate=cost(HALO_COST),
        name="inner",
    )(*handled)
    msg_shapes = [full(6 * tiles + 1), full(3 * tiles + 1)]
    own_shapes = [full(6 * tiles + 1), full(9 * tiles + 2)]
    msg, *own = pl.pallas_call(
        functools.partial(second_kernel, stages),
        in_specs=[VMEM] * 4,
        out_specs=[VMEM] * (1 + (stages == 1)),
        out_shape=[msg_shapes[1], own_shapes[1]] if stages == 1 else msg_shapes[:1],
        scratch_shapes=[pltpu.VMEM((7 * ny, nz), F32)],
        compiler_params=params(),
        cost_estimate=cost(FACE_COST),
        name="interface",
    )(got_a, got_b, inner, scalars)
    other = swap(msg, "gx", partner_by(devices, 1), crossed and stages == 1)
    for stage in range(stages - 1):
        closing_next = stage + 2 == stages
        msg, *own = pl.pallas_call(
            functools.partial(join_kernel, stage, stages, tiles),
            in_specs=[VMEM, VMEM, ANY] + [VMEM] * len(own),
            out_specs=[VMEM] * 2,
            out_shape=[msg_shapes[closing_next], own_shapes[closing_next]],
            compiler_params=params(),
            cost_estimate=cost(JOIN_COST),
            name="join",
        )(msg, other, rhs, *own)
        other = swap(msg, "gx", partner_by(devices, 2 << stage), crossed and closing_next)
    own = own[0]
    if crossed:
        own, _ = swap_whole(own, "gz")
    rhs = pl.pallas_call(
        functools.partial(edge_kernel, nx),
        in_specs=[VMEM] * 2,
        out_specs=VMEM,
        out_shape=vec(3, cells + ny),
        input_output_aliases={0: 0},
        compiler_params=params(),
        cost_estimate=cost(EDGE_COST),
        name="edge",
    )(rhs, far_b)
    _, ahead, behind = pl.pallas_call(
        functools.partial(sums_kernel, nx),
        in_specs=[VMEM] * 3,
        out_specs=[VMEM] * 3,
        out_shape=[vec(3, cells + ny)] + [full(3, nx, tiles)] * 2,
        input_output_aliases={0: 0},
        compiler_params=params(),
        cost_estimate=cost(SUMS_COST),
        name="sums",
    )(rhs, far_a, coefs)
    updated = pl.pallas_call(
        functools.partial(last_kernel, stages, parts),
        in_specs=[VMEM] * 6,
        out_specs=HBM,
        out_shape=full(3, nx, tiles),
        scratch_shapes=[
            pltpu.VMEM((3, nx, tiles, ROWS, nz), F32),
            pltpu.SemaphoreType.DMA((3 * parts,)),
        ],
        compiler_params=params(),
        name="solve",
    )(ahead, behind, coefs, scalars, other, own)
    return updated.reshape(3, nx, ny, nz)


def solution(mesh):
    placed = (P("gx", "gy", "gz"), P(None, "gx", "gy", "gz"), P("gx"))
    return jax.shard_map(
        on_device, mesh=mesh, in_specs=placed, out_specs=P(None, "gx", "gy", "gz"), check_vma=False
    )
```

```python
import functools

import jax
import jax.numpy as jnp
from jax import lax
from jax.experimental import pallas as pl
from jax.experimental.pallas import tpu as pltpu
from jax.sharding import PartitionSpec as P

time_step = 0.2
scale = time_step / 60.0
ROWS = 8
RHS_COST, SUMS_COST, JOIN_COST, EDGE_COST, FACE_COST, PACK_COST, HALO_COST = 60, 200, 20, 20000, 200000, 200000, 20
F32 = jnp.float32
VMEM = pl.BlockSpec(memory_space=pltpu.VMEM)
ANY = pl.BlockSpec(memory_space=pl.ANY)
HBM = pl.BlockSpec(memory_space=pltpu.HBM)


def pairing(count, odd):
    pairs = []
    for low in range(1 if odd else 0, count, 2):
        high = (low + 1) % count
        pairs += [(low, high), (high, low)]
    return pairs


def partner_by(count, step):
    return [(i, i ^ step) for i in range(count)]


def shifted_z(own, low, high, k):
    nz = own.shape[-1]
    if nz % 128 == 0:
        lane = lax.broadcasted_iota(jnp.int32, own.shape, own.ndim - 1)
        if k > 0:
            return pltpu.roll(jnp.where(lane < k, high, own), nz - k, own.ndim - 1)
        return pltpu.roll(jnp.where(lane >= nz + k, low, own), -k, own.ndim - 1)
    if k > 0:
        return jnp.concatenate([own[..., k:], high[..., :k]], -1)
    return jnp.concatenate([low[..., nz + k :], own[..., : nz + k]], -1)


def sixth(take):
    return 45.0 * (take(1) - take(-1)) - 9.0 * (take(2) - take(-2)) + (take(3) - take(-3))


def sixth_z(own, low, high):
    return sixth(lambda k: shifted_z(own, low, high, k))


def join(left, right):
    inv_delta = 1.0 / (right[5] + right[2] + left[3])
    jump = (right[0] - left[1]) * inv_delta
    from_in = left[4] * inv_delta
    from_out = right[4] * inv_delta
    group = (
        left[0] + left[4] * jump,
        right[1] - right[4] * jump,
        left[2] - left[4] * from_in,
        right[3] - right[4] * from_out,
        left[4] * from_out,
        left[5],
        right[6],
    )
    return group, (jump, from_in, from_out)


def pick(cond, yes, no):
    return tuple(jnp.where(cond, a, b) for a, b in zip(yes, no))


def join_own(is_left, own, other, forms):
    left = pick(is_left, own, other)
    right = pick(is_left, other, own)
    group, (jump, from_in, from_out) = join(left, right)
    new = []
    for c0, c1, c2 in forms:
        through = jnp.where(is_left, c2, c1)
        new.append(
            (
                c0 + through * jump,
                jnp.where(is_left, c1, 0.0) + through * from_in,
                jnp.where(is_left, 0.0, c2) + through * from_out,
            )
        )
    return group, new


def closing(is_left, group, forms):
    first, last, alpha, beta, m, inv_first, inv_last = group
    kappa = 1.0 / jnp.where(is_left, inv_first + alpha, inv_last + beta)
    outer = jnp.where(is_left, first, -last) * kappa
    gain = kappa * m
    facing = jnp.where(is_left, last - m * outer, first + m * outer)
    resist = jnp.where(is_left, beta, alpha + inv_first) - m * gain
    out = []
    for c0, c1, c2 in forms:
        far = jnp.where(is_left, c1, c2)
        near = jnp.where(is_left, c2, c1)
        out.append((c0 + far * outer, far * gain + near))
    return facing, resist, out


def put_scalars(ref, block, values):
    for row, value in enumerate(values):
        ref[block, row : row + 1] = value


def get_scalars(ref, block, count):
    return [ref[block, row : row + 1] for row in range(count)]


def store_group(ref, group, tiles):
    for f in range(3):
        ref[f * tiles : (f + 1) * tiles] = group[0][f]
        ref[(3 + f) * tiles : (4 + f) * tiles] = group[1][f]
    put_scalars(ref, 6 * tiles, group[2:])


def load_group(ref, tiles):
    shape = (3, tiles) + ref.shape[1:]
    first = ref[: 3 * tiles].reshape(shape)
    last = ref[3 * tiles : 6 * tiles].reshape(shape)
    return (first, last, *get_scalars(ref, 6 * tiles, 5))


def store_closing(msg_ref, own_ref, facing, resist, out, tiles):
    own_ref[6 * tiles + 1 : 9 * tiles + 1] = facing.reshape((3 * tiles,) + facing.shape[2:])
    put_scalars(own_ref, 9 * tiles + 1, [resist])
    for f in range(3):
        msg_ref[f * tiles : (f + 1) * tiles] = facing[f]
        own_ref[f * tiles : (f + 1) * tiles] = out[0][0][f]
        own_ref[(3 + f) * tiles : (4 + f) * tiles] = out[1][0][f]
    put_scalars(msg_ref, 3 * tiles, [resist])
    put_scalars(own_ref, 6 * tiles, [out[0][1], out[1][1]])


def store_forms(ref, forms, tiles):
    for f in range(3):
        ref[f * tiles : (f + 1) * tiles] = forms[0][0][f]
        ref[(3 + f) * tiles : (4 + f) * tiles] = forms[1][0][f]
    put_scalars(ref, 6 * tiles, [*forms[0][1:], *forms[1][1:]])


def load_forms(ref, tiles):
    shape = (3, tiles) + ref.shape[1:]
    scalars = get_scalars(ref, 6 * tiles, 4)
    return [
        (ref[: 3 * tiles].reshape(shape), scalars[0], scalars[1]),
        (ref[3 * tiles : 6 * tiles].reshape(shape), scalars[2], scalars[3]),
    ]


def sums_at(ny, side, k):
    start = (2 * k + side) * ny
    return slice(start, start + ny)


def pick_edges(ref_a, ref_b, take):
    odd = lax.rem(lax.axis_index("gy"), 2)
    for ref, high in ((ref_a, 1 - odd), (ref_b, odd)):
        take(ref, high)


def first_kernel(
    chunks, faces, density, momentum,
    rho_v, mom_v, flux_y, flux_z, sums, small_b, small_a, coefs, scalars,
    face_s, sems,
):
    nx = faces.shape[0]
    nz = density.shape[1]
    ny = density.shape[0] // nx
    tiles = ny // ROWS
    face_copy = pltpu.make_async_copy(faces, face_s, sems.at[0])
    face_copy.start()
    step = nx * ny // chunks
    copies = []
    for c in range(chunks):
        at = pl.ds(c * step, step)
        copies.append(
            (
                pltpu.make_async_copy(density.at[at], rho_v.at[at], sems.at[1 + 2 * c]),
                pltpu.make_async_copy(momentum.at[:, at], mom_v.at[:, at], sems.at[2 + 2 * c]),
            )
        )
        for copy in copies[-1]:
            copy.start()
    tile = (ROWS, nz)
    pitch = ny + ROWS
    for line in range(3 * nx + 1):
        flux_y[line * pitch : line * pitch + ROWS] = jnp.zeros(tile, F32)
    face_copy.wait()
    inv = [1.0 / jnp.full(tile, face_s[i], F32) for i in range(nx)]
    phi = [jnp.ones(tile, F32)]
    flux = phi[0]
    for i in range(1, nx):
        phi.append(phi[-1] + flux * inv[i])
        flux = flux + phi[-1]
    m = 1.0 / flux
    psi = [jnp.ones(tile, F32)]
    flux = psi[0]
    for i in range(nx - 1, 0, -1):
        psi.append(psi[-1] + flux * inv[i])
        flux = flux + psi[-1]
    psi = psi[::-1]
    for i in range(nx):
        coefs[i] = phi[i]
        coefs[nx + i] = psi[i] * m
    scalars[0:1] = (psi[0] * m)[0:1]
    scalars[1:2] = (phi[nx - 1] * m)[0:1]
    scalars[2:3] = m[0:1]
    scalars[3:4] = inv[0][0:1]
    scalars[4:5] = inv[nx - 1][0:1]
    scalars[5:8] = jnp.zeros((3, nz), F32)
    total = [[None] * 6, [None] * 6]
    for x in range(nx):
        if x % (nx // chunks) == 0:
            for copy in copies[x // (nx // chunks)]:
                copy.wait()
        at = slice(x * ny, (x + 1) * ny)
        rho, m0, m1 = [b.reshape(tiles, ROWS, nz) for b in (rho_v[at], mom_v[0, at], mom_v[1, at])]
        inv_rho = 1.0 / rho
        v0, v1 = m0 * inv_rho, m1 * inv_rho
        values = (m0, m0 * v0, m0 * v1, rho, m1, m1 * v1)
        for side, weight in enumerate((coefs[nx + x], coefs[x])):
            for k, value in enumerate(values):
                term = weight * value
                total[side][k] = term if x == 0 else total[side][k] + term
        for f in range(3):
            start = (f * nx + x) * pitch + ROWS
            flux_y[start : start + ny] = values[f].reshape(ny, nz)
            flux_z[f * nx * ny + x * ny : f * nx * ny + (x + 1) * ny] = values[(4, 2, 5)[f]].reshape(ny, nz)
    for side in range(2):
        for k in range(6):
            sums[sums_at(ny, side, k)] = total[side][k].reshape(ny, nz)

    def take_small(ref, high):
        sign = jnp.where(high == 1, scale, -scale)
        n1, n2, n3 = [
            sums[pl.ds(high * (ny - 1) + (1 - 2 * high) * k, 6, stride=ny)] * sign for k in range(3)
        ]
        ref[...] = jnp.zeros((3 * ROWS, nz), F32)
        ref[0:6] = 45.0 * n1 - 9.0 * n2 + n3
        ref[ROWS : ROWS + 6] = n2 - 9.0 * n1
        ref[2 * ROWS : 2 * ROWS + 6] = n1

    pick_edges(small_a, small_b, take_small)


def pack_kernel(nx, second, rho_v, mom_v, ref):
    ny = rho_v.shape[0] // (nx + 1)
    odd = lax.rem(lax.axis_index("gy"), 2)
    high = odd if second else 1 - odd
    sign = jnp.where(high == 1, scale, -scale)
    rows = [pl.ds(high * (ny - 1) + (1 - 2 * high) * k, nx, stride=ny) for k in range(3)]
    m0, m1, v0 = [], [], []
    for at in rows:
        m0.append(mom_v[0, at])
        m1.append(mom_v[1, at])
        v0.append(m0[-1] / rho_v[at] * sign)
    for f in range(3):
        n1, n2, n3 = [(m0[k] * sign, m0[k] * v0[k], m1[k] * v0[k])[f] for k in range(3)]
        ref[3 * f] = 45.0 * n1 - 9.0 * n2 + n3
        ref[3 * f + 1] = n2 - 9.0 * n1
        ref[3 * f + 2] = n1


def z_slots(nz, tile):
    per = nz // 6
    return tile // per, 6 * (tile % per) + 3


def packed_rows(nz, tiles):
    return (z_slots(nz, tiles - 1)[0] + 1) * ROWS


def pack_z(sums, flux_z, message):
    nz = sums.shape[1]
    first = sums.shape[0]
    message[:first] = sums[...]
    lane = lax.broadcasted_iota(jnp.int32, (ROWS, nz), 1)
    packed = {}
    for tile in range(flux_z.shape[0] // ROWS):
        group, shift = z_slots(nz, tile)
        moved = pltpu.roll(flux_z[tile * ROWS : (tile + 1) * ROWS], shift, 1)
        packed[group] = jnp.where(lane < shift - 3, packed[group], moved) if group in packed else moved
    for group, value in packed.items():
        message[first + group * ROWS : first + (group + 1) * ROWS] = value


def unpack_z(message, first, tile):
    nz = message.shape[1]
    group, shift = z_slots(nz, tile)
    return pltpu.roll(message[first + group * ROWS : first + (group + 1) * ROWS], nz - shift, 1)


def halos_y(is_odd, from_a, from_b):
    low = jnp.where(is_odd, from_a, from_b)
    high = jnp.where(is_odd, from_b, from_a)
    return low, high


def inner_kernel(ny, sums, sums_low, sums_high, inner, pad):
    nz = sums.shape[1]
    pad[0:ROWS] = jnp.zeros((ROWS, nz), F32)
    pad[ROWS + ny : 2 * ROWS + ny] = jnp.zeros((ROWS, nz), F32)
    for side in range(2):
        for f, (state, along_y, along_z) in enumerate(((3, 0, 4), (0, 1, 2), (4, 2, 5))):
            pad[ROWS : ROWS + ny] = sums[sums_at(ny, side, along_y)]
            dy = sixth(lambda s: pad[ROWS + s : ROWS + s + ny])
            dz = sixth_z(*[r[sums_at(ny, side, along_z)] for r in (sums, sums_low, sums_high)])
            inner[sums_at(ny, side, f)] = sums[sums_at(ny, side, state)] - scale * (dy + dz)


def second_kernel(stages, small_a, small_b, inner, scalars, *refs):
    ny, nz = inner.shape[0] // 6, inner.shape[1]
    tiles = ny // ROWS
    block = refs[-1]
    is_odd = lax.rem(lax.axis_index("gy"), 2) == 1
    low, high = halos_y(is_odd, small_a[...], small_b[...])
    alpha, beta, m, inv_first, inv_last = [scalars[i : i + 1] for i in range(5)]
    block[0 : 6 * ny] = inner[...]
    for k in range(3):
        for row, edge in ((k, low), (ny - 1 - k, high)):
            at = pl.ds(row, 6, stride=ny)
            block[at] = block[at] + edge[k * ROWS : k * ROWS + 6]
    values = [block[sums_at(ny, side, f)].reshape(tiles, ROWS, nz) for side in range(2) for f in range(3)]
    first = jnp.stack(values[:3])
    last = jnp.stack(values[3:]) * m
    group = (first, last, alpha, beta, m, inv_first, inv_last)
    if stages == 1:
        is_left = lax.rem(lax.axis_index("gx"), 2) == 0
        zero = jnp.zeros_like(first)
        one = jnp.ones_like(alpha)
        forms = [(zero, one, 0.0 * one), (zero, 0.0 * one, one)]
        facing, resist, out = closing(is_left, group, forms)
        store_closing(refs[0], refs[1], facing, resist, out, tiles)
    else:
        store_group(refs[0], group, tiles)


def join_kernel(stage, stages, tiles, *refs):
    refs = refs[:2] + refs[3:]
    if stage == 0:
        mine, other, msg, own = refs
        shape = (3, tiles) + mine.shape[1:]
        zero, one = jnp.zeros(shape, F32), jnp.ones((1, shape[-1]), F32)
        forms = [(zero, one, 0.0 * one), (zero, 0.0 * one, one)]
    else:
        mine, other, forms_ref, msg, own = refs
        forms = load_forms(forms_ref, tiles)
    at = lax.axis_index("gx")
    is_left = lax.rem(lax.div(at, 1 << stage), 2) == 0
    group, forms = join_own(is_left, load_group(mine, tiles), load_group(other, tiles), forms)
    if stage + 2 == stages:
        is_left = lax.rem(lax.div(at, 2 << stage), 2) == 0
        facing, resist, out = closing(is_left, group, forms)
        store_closing(msg, own, facing, resist, out, tiles)
    else:
        store_group(msg, group, tiles)
        store_forms(own, forms, tiles)


def rhs_kernel(nx, density, momentum, flux_y, flux_z, *refs):
    ny = density.shape[0] // (nx + 1)
    pitch = ny + ROWS
    if len(refs) == 3:
        message, rhs, unpacked = refs
        for tile in range(unpacked.shape[0] // ROWS):
            unpacked[tile * ROWS : (tile + 1) * ROWS] = unpack_z(message, 12 * ny, tile)
        flux_z_low = flux_z_high = unpacked
    else:
        flux_z_low, flux_z_high, rhs, _ = refs
    for f in range(3):
        for x in range(nx):
            at = (f * nx + x) * pitch + ROWS
            dy = sixth(lambda s: flux_y[at + s : at + s + ny])
            lines = slice((f * nx + x) * ny, (f * nx + x + 1) * ny)
            dz = sixth_z(*[r[lines] for r in (flux_z, flux_z_low, flux_z_high)])
            cells = slice(x * ny, (x + 1) * ny)
            state = density[cells] if f == 0 else momentum[f - 1, cells]
            rhs[f, cells] = state - scale * (dy + dz)


def add_edge(nx, rhs, edge, high):
    ny = rhs.shape[1] // (nx + 1)
    for f in range(3):
        for k in range(3):
            at = pl.ds(high * (ny - 1) + (1 - 2 * high) * k, nx, stride=ny)
            rhs[f, at] = rhs[f, at] + edge[3 * f + k]


def edge_kernel(nx, rhs_in, edge_b, rhs):
    rhs[...] = rhs_in[...]
    add_edge(nx, rhs, edge_b, lax.rem(lax.axis_index("gy"), 2))


def sums_kernel(nx, rhs_in, edge_a, coefs, rhs, ahead, behind):
    ny, nz = rhs.shape[1] // (nx + 1), rhs.shape[2]
    shape = (ny // ROWS, ROWS, nz)
    rhs[...] = rhs_in[...]
    add_edge(nx, rhs, edge_a, 1 - lax.rem(lax.axis_index("gy"), 2))
    for f in range(3):
        total = None
        for x in range(nx):
            r = rhs[f, x * ny : (x + 1) * ny].reshape(shape)
            total = coefs[x] * r if x == 0 else total + coefs[x] * r
            ahead[f, x] = total
        total = jnp.zeros(shape, F32)
        for x in range(nx - 1, -1, -1):
            behind[f, x] = total
            if x > 0:
                r = rhs[f, x * ny : (x + 1) * ny].reshape(shape)
                total = total + coefs[nx + x] * r


def last_kernel(stages, parts, ahead, behind, coefs, scalars, other, own, updated, out_v, sems):
    _, nx, tiles, _, nz = ahead.shape
    is_left = lax.rem(lax.div(lax.axis_index("gx"), 1 << (stages - 1)), 2) == 0
    sign = jnp.where(is_left, 1.0, -1.0)
    inv = sign / (own[9 * tiles + 1, 0:1] + other[3 * tiles, 0:1])
    m = scalars[2:3]
    copies = []
    for f in range(3):
        at = slice(f * tiles, (f + 1) * tiles)
        mid = (other[at] - own[(6 + f) * tiles + 1 : (7 + f) * tiles + 1]) * inv
        jin = own[at] + own[6 * tiles, 0:1] * mid
        jout = m * (own[(3 + f) * tiles : (4 + f) * tiles] + own[6 * tiles, 1:2] * mid)
        for x in range(nx):
            out_v[f, x] = coefs[nx + x] * (ahead[f, x] - jin) + coefs[x] * (behind[f, x] + jout)
            if (x + 1) % (nx // parts) == 0:
                part = pl.ds(x + 1 - nx // parts, nx // parts)
                copy = pltpu.make_async_copy(out_v.at[f, part], updated.at[f, part], sems.at[len(copies)])
                copy.start()
                copies.append(copy)
    for copy in copies:
        copy.wait()


def params(limit=48):
    return pltpu.CompilerParams(vmem_limit_bytes=limit * 1024 * 1024)


def swap(block, axis, pairs, crossed):
    if not crossed:
        return lax.ppermute(block, axis, pairs)
    both = [(2 * a + c, 2 * b + 1 - c) for a, b in pairs for c in range(2)]
    return lax.ppermute(block, (axis, "gz"), both)


def swap_edges(block_a, block_b, crossed=False):
    count = lax.axis_size("gy")
    return (
        swap(block_a, "gy", pairing(count, False), crossed),
        swap(block_b, "gy", pairing(count, True), crossed),
    )


def swap_whole(block, axis):
    count = lax.axis_size(axis)
    if count == 2:
        got = lax.ppermute(block, axis, pairing(2, False))
        return got, got
    ring = [(i, (i + 1) % count) for i in range(count)]
    return lax.ppermute(block, axis, ring), lax.ppermute(block, axis, [(b, a) for a, b in ring])


def on_device(density, momentum, lower_face):
    nx, ny, nz = density.shape
    tiles = ny // ROWS
    cells = nx * ny
    chunks, parts = (4 if nx % 4 == 0 else 1), (2 if nx % 2 == 0 else 1)
    devices = lax.axis_size("gx")
    stages = (devices - 1).bit_length()
    crossed = lax.axis_size("gz") == 2
    full = lambda *lead: jax.ShapeDtypeStruct(lead + (ROWS, nz), F32)
    vec = lambda *lead: jax.ShapeDtypeStruct(lead + (nz,), F32)
    cost = lambda n: pl.CostEstimate(flops=n * cells * nz, bytes_accessed=n * cells * nz, transcendentals=0)
    inputs = (lower_face, density.reshape(cells, nz), momentum.reshape(2, cells, nz))
    inputs = [pltpu.with_memory_space_constraint(x, pltpu.HBM) for x in inputs]
    density, momentum, flux_y, flux_z, sums, small_b, small_a, coefs, scalars = pl.pallas_call(
        functools.partial(first_kernel, chunks),
        in_specs=[HBM] * 3,
        out_specs=[VMEM] * 9,
        out_shape=[
            vec(cells + ny),
            vec(2, cells + ny),
            vec(3 * nx * (ny + ROWS) + ROWS),
            vec(3 * cells),
            vec(12 * ny),
            vec(3 * ROWS),
            vec(3 * ROWS),
            full(2 * nx),
            full(),
        ],
        scratch_shapes=[pltpu.SMEM((nx,), F32), pltpu.SemaphoreType.DMA((1 + 2 * chunks,))],
        compiler_params=params(),
        name="load",
    )(*inputs)
    got_a, got_b = swap_edges(small_a, small_b, crossed)
    packed = crossed and nz % 128 == 0
    z_rows = 12 * ny + packed_rows(nz, 3 * cells // ROWS)

    edge_a, edge_b = [
        pl.pallas_call(
            functools.partial(pack_kernel, nx, second),
            in_specs=[VMEM] * 2,
            out_specs=VMEM,
            out_shape=vec(9, nx),
            compiler_params=params(),
            cost_estimate=cost(PACK_COST),
            name="pack",
        )(density, momentum)
        for second in (False, True)
    ]
    if packed:
        z_message = pl.pallas_call(
            pack_z,
            in_specs=[VMEM] * 2,
            out_specs=VMEM,
            out_shape=vec(z_rows),
            compiler_params=params(),
            cost_estimate=cost(RHS_COST),
            name="pack_z",
        )(sums, flux_z)
        z_low, z_high = swap_whole(z_message, "gz")
        handled = (z_low, sums, sums)
        beyond = (z_low,)
    else:
        sums_low, sums_high = swap_whole(sums, "gz")
        beyond = swap_whole(flux_z, "gz")
        handled = (sums_low, sums, sums) if crossed else (sums, sums_low, sums_high)
    far_a, far_b = swap_edges(edge_a, edge_b)
    rhs = pl.pallas_call(
        functools.partial(rhs_kernel, nx),
        in_specs=[VMEM] * (4 + len(beyond)),
        out_specs=VMEM,
        out_shape=vec(3, cells + ny),
        scratch_shapes=[pltpu.VMEM((3 * cells, nz), F32)],
        compiler_params=params(),
        cost_estimate=cost(RHS_COST),
        name="rhs",
    )(density, momentum, flux_y, flux_z, *beyond)
    inner = pl.pallas_call(
        functools.partial(inner_kernel, ny),
        in_specs=[VMEM] * 3,
        out_specs=VMEM,
        out_shape=vec(6 * ny),
        scratch_shapes=[pltpu.VMEM((ny + 2 * ROWS, nz), F32)],
        compiler_params=params(),
        cost_estimate=cost(HALO_COST),
        name="inner",
    )(*handled)
    msg_shapes = [full(6 * tiles + 1), full(3 * tiles + 1)]
    own_shapes = [full(6 * tiles + 1), full(9 * tiles + 2)]
    msg, *own = pl.pallas_call(
        functools.partial(second_kernel, stages),
        in_specs=[VMEM] * 4,
        out_specs=[VMEM] * (1 + (stages == 1)),
        out_shape=[msg_shapes[1], own_shapes[1]] if stages == 1 else msg_shapes[:1],
        scratch_shapes=[pltpu.VMEM((7 * ny, nz), F32)],
        compiler_params=params(),
        cost_estimate=cost(FACE_COST),
        name="interface",
    )(got_a, got_b, inner, scalars)
    other = swap(msg, "gx", partner_by(devices, 1), crossed and stages == 1)
    for stage in range(stages - 1):
        closing_next = stage + 2 == stages
        msg, *own = pl.pallas_call(
            functools.partial(join_kernel, stage, stages, tiles),
            in_specs=[VMEM, VMEM, ANY] + [VMEM] * len(own),
            out_specs=[VMEM] * 2,
            out_shape=[msg_shapes[closing_next], own_shapes[closing_next]],
            compiler_params=params(),
            cost_estimate=cost(JOIN_COST),
            name="join",
        )(msg, other, rhs, *own)
        other = swap(msg, "gx", partner_by(devices, 2 << stage), crossed and closing_next)
    own = own[0]
    if crossed:
        own, _ = swap_whole(own, "gz")
    rhs = pl.pallas_call(
        functools.partial(edge_kernel, nx),
        in_specs=[VMEM] * 2,
        out_specs=VMEM,
        out_shape=vec(3, cells + ny),
        input_output_aliases={0: 0},
        compiler_params=params(),
        cost_estimate=cost(EDGE_COST),
        name="edge",
    )(rhs, far_b)
    _, ahead, behind = pl.pallas_call(
        functools.partial(sums_kernel, nx),
        in_specs=[VMEM] * 3,
        out_specs=[VMEM] * 3,
        out_shape=[vec(3, cells + ny)] + [full(3, nx, tiles)] * 2,
        input_output_aliases={0: 0},
        compiler_params=params(),
        cost_estimate=cost(SUMS_COST),
        name="sums",
    )(rhs, far_a, coefs)
    updated = pl.pallas_call(
        functools.partial(last_kernel, stages, parts),
        in_specs=[VMEM] * 6,
        out_specs=HBM,
        out_shape=full(3, nx, tiles),
        scratch_shapes=[
            pltpu.VMEM((3, nx, tiles, ROWS, nz), F32),
            pltpu.SemaphoreType.DMA((3 * parts,)),
        ],
        compiler_params=params(),
        name="solve",
    )(ahead, behind, coefs, scalars, other, own)
    return updated.reshape(3, nx, ny, nz)


def solution(mesh):
    placed = (P("gx", "gy", "gz"), P(None, "gx", "gy", "gz"), P("gx"))
    return jax.shard_map(
        on_device, mesh=mesh, in_specs=placed, out_specs=P(None, "gx", "gy", "gz"), check_vma=False
    )
```
